128 devices in a mesh: blk: 16 (over z, y_lo, core), rep: 8 (over y_hi, x).
Axes of the slice: x: 4, y: 4 (y_hi: 2, y_lo: 2; y = y_hi * 2 + y_lo), z: 4, core: 2. Of those that a mesh axis runs over, the one named last changes fastest.
Arguments:
- features: bfloat16 [131072, 256], P(('blk', 'rep'))
- weight: bfloat16 [256, 256], replicated, may hold values from -0.375 to 0.375
- norm_gain: float32 [256], replicated, may hold values from 0.1 to 1.9
- norm_shift: float32 [256], replicated, may hold values from -3 to 3
- tile_values: bfloat16 [16, 128, 32, 128, 128], P('blk', 'rep'), may hold values from 0 to 0.0625
- tile_rows: int32 [16, 128, 32], P('blk', 'rep'), may hold values from 0 to 63
- tile_cols: int32 [16, 128, 32], P('blk', 'rep'), may hold values from 0 to 7
- tile_counts: int32 [16, 128], P('blk', 'rep'), may hold values from 8 to 32, as said below
- cotangent: bfloat16 [131072, 256], P(('blk', 'rep')), may hold values from -6 to 6
Outputs:
- output: bfloat16 [131072, 256], P(('blk', 'rep'))
- grad_x: bfloat16 [131072, 256], P(('blk', 'rep'))
- grad_w: float32 [256, 256], replicated
- grad_gamma: float32 [256], replicated
- grad_beta: float32 [256], replicated
The draws below stay inside these ranges and needn't reach their ends.
Inputs may be any that keep to these rules, and one draw needn't show every extreme that they name: `tile_counts`: A device's count for its own position along blk is 32.
All inputs are finite; a program needn't handle non-finite values.
Results may differ from the reference program's by a relative error of at most 0.024.
Values may be sent and summed in bfloat16 or wider, within the bound.
No kernel may reach another device: no remote copies, remote signals or barrier semaphores. Data moves between devices by JAX's collectives and lax.ppermute only.
A program may use at most 192 MiB of HBM per device.

```python
import jax
import jax.numpy as jnp
from jax import lax

F = 256
TILE = 128
R = 1024
KB = 32
NODES = 131072
N_BLK = 16
N_REP = 8


def draw_features(key, part):
    key = jax.random.fold_in(key, 11)
    key_base, key_scale, key_shared = jax.random.split(key, 3)
    node_count = R * N_BLK * N_REP
    position = jnp.arange(node_count, dtype=jnp.float32)[:, None]
    rising = 1.0 + 2.0 * position / (node_count - 1)
    spread = 10.0 ** jax.random.uniform(key_scale, (node_count, 1), dtype=jnp.float32)
    base = jax.random.normal(key_base, (node_count, F), dtype=jnp.float32)
    base = base + 0.12 * jax.random.normal(key_shared, (1, F), dtype=jnp.float32)
    return (0.3 * base * spread * rising).astype(jnp.bfloat16)


def draw_tile_counts(key, part):
    key = jax.random.fold_in(key, 23)
    counts = jax.random.randint(key, (N_BLK, N_REP * N_BLK), KB // 4, KB + 1, dtype=jnp.int32)
    own_slot = jnp.arange(N_REP * N_BLK, dtype=jnp.int32)[None, :] % N_BLK == jnp.arange(N_BLK, dtype=jnp.int32)[:, None]
    return jnp.where(own_slot, KB, counts).astype(jnp.int32)


def draw_cotangent(key, part):
    key = jax.random.fold_in(key, 37)
    key_base, key_shared = jax.random.split(key)
    node_count = R * N_BLK * N_REP
    base = jax.random.normal(key_base, (node_count, F), dtype=jnp.float32)
    offset = 0.3 * jax.random.normal(key_shared, (1, F), dtype=jnp.float32)
    return jnp.clip(base + offset, -6.0, 6.0).astype(jnp.bfloat16)


def set_ends(values, own_key, least, top_value):
    spot = [jax.random.randint(jax.random.fold_in(own_key, axis), (), 0, length) for axis, length in enumerate(values.shape)]
    longest = values.shape.index(max(values.shape))
    beside = spot[:longest] + [(spot[longest] + 1) % values.shape[longest]] + spot[longest + 1:]
    return values.at[tuple(spot)].set(least).at[tuple(beside)].set(top_value)


def block_scale(own_key, extent, cuts, low, top_value):
    level = 1.0
    for dim, parts in cuts:
        draws = jax.random.uniform(jax.random.fold_in(jax.random.fold_in(own_key, 6), dim), (parts,), jnp.float32, low / len(cuts), top_value / len(cuts))
        level = level * jnp.repeat(jnp.exp(draws), extent[dim] // parts).reshape((-1,) + (1,) * (len(extent) - 1 - dim))
    return level


def noise(rng, extent, deviation, bound, kind=jnp.bfloat16):
    return jnp.clip(deviation * jax.random.normal(rng, extent, jnp.float32), -bound, bound).astype(kind)


def setup_inputs(seed: int = 0) -> dict:
    streams_of = jax.random.split(jax.random.key(seed), 10)
    return {
        "features": draw_features(jax.random.fold_in(streams_of[9], 71), 0),
        "weight": noise(streams_of[1], (F, F), F ** -0.5, 0.375),
        "norm_gain": jnp.clip(1.0 + 0.18 * jax.random.normal(streams_of[2], (F,), jnp.float32), 0.1, 1.9),
        "norm_shift": noise(streams_of[3], (F,), 0.5, 3.0, jnp.float32),
        "tile_values": jnp.clip(0.0625 * jax.random.uniform(streams_of[4], (N_BLK, N_REP * N_BLK, KB, TILE, TILE), jnp.float32) ** block_scale(streams_of[4], (N_BLK, N_REP * N_BLK, KB, TILE, TILE), ((0, 16), (1, 8)), -0.2, 0.2), 0.0, 0.0625).astype(jnp.bfloat16),
        "tile_rows": set_ends(jax.random.randint(streams_of[5], (N_BLK, N_REP * N_BLK, KB), 0, N_REP * R // TILE), jax.random.fold_in(streams_of[5], 1), 0, (N_REP * R // TILE) - 1).astype(jnp.int32),
        "tile_cols": set_ends(jax.random.randint(streams_of[6], (N_BLK, N_REP * N_BLK, KB), 0, R // TILE), jax.random.fold_in(streams_of[6], 1), 0, (R // TILE) - 1).astype(jnp.int32),
        "tile_counts": draw_tile_counts(jax.random.fold_in(streams_of[9], 71), 0),
        "cotangent": draw_cotangent(jax.random.fold_in(streams_of[9], 71), 0),
    }


norm_eps = 1e-05

def device_tiles(device, tile_values, tile_rows, tile_cols, tile_counts):
    blk_pos = device // N_REP
    rep_pos = device % N_REP
    col_count = R // TILE
    blocks = lax.dynamic_index_in_dim(tile_values, blk_pos, 0, keepdims=False)
    blocks = lax.dynamic_slice_in_dim(blocks, rep_pos * N_BLK, N_BLK, 0).astype(jnp.float32)
    row_lists = lax.dynamic_slice_in_dim(lax.dynamic_index_in_dim(tile_rows, blk_pos, 0, keepdims=False), rep_pos * N_BLK, N_BLK, 0)
    col_lists = lax.dynamic_slice_in_dim(lax.dynamic_index_in_dim(tile_cols, blk_pos, 0, keepdims=False), rep_pos * N_BLK, N_BLK, 0)
    live_counts = lax.dynamic_slice_in_dim(lax.dynamic_index_in_dim(tile_counts, blk_pos, 0, keepdims=False), rep_pos * N_BLK, N_BLK, 0)
    sources = jnp.arange(N_BLK, dtype=jnp.int32)[:, None]
    global_cols = ((sources * N_REP + rep_pos) * col_count + col_lists).astype(jnp.int32)
    global_rows = (blk_pos * N_REP * col_count + row_lists).astype(jnp.int32)
    live_mask = (jnp.arange(KB, dtype=jnp.int32)[None, :] < live_counts[:, None]).astype(jnp.float32)
    return (blocks * live_mask[:, :, None, None], global_rows, global_cols)

def reference(features, weight, norm_gain, norm_shift, tile_values, tile_rows, tile_cols, tile_counts, cotangent):
    node_count = NODES
    tile_total = node_count // TILE
    proj = jnp.dot(features, weight, preferred_element_type=jnp.float32).astype(jnp.bfloat16)
    proj_tiles = proj.reshape(tile_total, TILE, F).astype(jnp.float32)
    devices = jnp.arange(N_BLK * N_REP, dtype=jnp.int32)

    def forward_step(running, device):
        blocks, global_rows, global_cols = device_tiles(device, tile_values, tile_rows, tile_cols, tile_counts)
        product = jnp.einsum('skij,skjf->skif', blocks, proj_tiles[global_cols])
        return (running.at[global_rows].add(product), None)
    start_sum = jnp.zeros((tile_total, TILE, F), jnp.float32)
    summed, unused = lax.scan(forward_step, start_sum, devices)
    summed = summed.reshape(node_count, F)
    feat_mean = lax.optimization_barrier(jnp.sum(summed, axis=0)) / node_count
    centered = summed - feat_mean
    variance = lax.optimization_barrier(jnp.sum(centered * centered, axis=0)) / node_count
    inv_std = lax.rsqrt(variance + norm_eps)
    normed = centered * inv_std
    affine = norm_gain * normed + norm_shift
    gate_value = jax.nn.sigmoid(affine)
    output = (affine * gate_value).astype(jnp.bfloat16)
    grad_affine = cotangent.astype(jnp.float32) * gate_value * (1.0 + affine * (1.0 - gate_value))
    grad_beta = lax.optimization_barrier(jnp.sum(grad_affine, axis=0))
    grad_gamma = lax.optimization_barrier(jnp.sum(grad_affine * normed, axis=0))
    grad_summed = (norm_gain * inv_std * (grad_affine - grad_beta / node_count - normed * grad_gamma / node_count)).astype(jnp.bfloat16)
    grad_tiles = grad_summed.reshape(tile_total, TILE, F).astype(jnp.float32)

    def backward_step(running, device):
        blocks, global_rows, global_cols = device_tiles(device, tile_values, tile_rows, tile_cols, tile_counts)
        product = jnp.einsum('skji,skjf->skif', blocks, grad_tiles[global_rows])
        return (running.at[global_cols].add(product), None)
    grad_proj, unused = lax.scan(backward_step, start_sum, devices)
    grad_proj = grad_proj.reshape(node_count, F).astype(jnp.bfloat16)
    grad_x = lax.dot_general(grad_proj, weight, (((1,), (1,)), ((), ())), preferred_element_type=jnp.float32).astype(jnp.bfloat16)
    grad_w = lax.dot_general(features, grad_proj, (((0,), (0,)), ((), ())), preferred_element_type=jnp.float32)
    return (output, grad_x, grad_w, grad_gamma, grad_beta)
```

```python
import functools

import jax
import jax.numpy as jnp
from jax import lax
from jax.experimental import pallas as pl
from jax.experimental.pallas import tpu as pltpu
from jax.sharding import PartitionSpec as P

norm_eps = 1e-05
GROUP = 8
BF16, F32 = jnp.bfloat16, jnp.float32
VMEM_LIMIT = 48 * 2**20


def forward_kernel(rows_ref, cols_ref, counts_ref, tiles_ref, proj_ref, out_ref, offset_ref, acc_ref):
    step = pl.program_id(0)
    row_tiles = out_ref.shape[0]

    @pl.when(step == 0)
    def _():
        def zero(i, carry):
            acc_ref[i] = jnp.zeros(acc_ref.shape[1:], F32)
            return carry

        lax.fori_loop(0, row_tiles + 1, zero, 0)

    count = counts_ref[step]

    def add_group(g, carry):
        products, where = [], []
        for j in range(GROUP):
            k = g * GROUP + j
            products.append(
                jnp.dot(tiles_ref[0, k], proj_ref[0, cols_ref[step, k]], preferred_element_type=F32)
            )
            where.append(jnp.where(k < count, rows_ref[step, k], row_tiles))
        for j in range(GROUP):
            acc_ref[where[j]] += products[j]
        return carry

    lax.fori_loop(0, (count + GROUP - 1) // GROUP, add_group, 0)

    @pl.when(step == pl.num_programs(0) - 1)
    def _():
        def total(i, carry):
            return carry + jnp.sum(acc_ref[i].reshape(-1, 8, acc_ref.shape[2]), axis=0)

        sums = lax.fori_loop(0, row_tiles, total, jnp.zeros((8, acc_ref.shape[2]), F32))
        offset = jnp.sum(sums, axis=0, keepdims=True) / (row_tiles * acc_ref.shape[1])
        offset_ref[...] = offset

        def put(i, carry):
            out_ref[i] = (acc_ref[i] - offset).astype(out_ref.dtype)
            return carry

        lax.fori_loop(0, row_tiles, put, 0)


def forward_tiles(tiles, rows, cols, counts, proj, row_tiles):
    sources, slots, tile, _ = tiles.shape
    col_tiles, width = proj.shape[1], proj.shape[3]
    return pl.pallas_call(
        forward_kernel,
        grid_spec=pltpu.PrefetchScalarGridSpec(
            num_scalar_prefetch=3,
            grid=(sources,),
            in_specs=[
                pl.BlockSpec((1, slots, tile, tile), lambda s, *_: (s, 0, 0, 0)),
                pl.BlockSpec((1, col_tiles, tile, width), lambda s, *_: (s, 0, 0, 0)),
            ],
            out_specs=[
                pl.BlockSpec((row_tiles, tile, width), lambda s, *_: (0, 0, 0)),
                pl.BlockSpec((1, width), lambda s, *_: (0, 0)),
            ],
            scratch_shapes=[pltpu.VMEM((row_tiles + 1, tile, width), F32)],
        ),
        out_shape=[
            jax.ShapeDtypeStruct((row_tiles, tile, width), BF16),
            jax.ShapeDtypeStruct((1, width), F32),
        ],
        compiler_params=pltpu.CompilerParams(vmem_limit_bytes=VMEM_LIMIT),
        name="forward_tiles",
    )(rows, cols, counts, tiles, proj)


def backward_kernel(rows_ref, cols_ref, counts_ref, tiles_ref, grad_ref, out_ref, acc_ref):
    step = pl.program_id(0)
    col_tiles = out_ref.shape[1]
    for i in range(col_tiles + 1):
        acc_ref[i] = jnp.zeros(acc_ref.shape[1:], F32)
    count = counts_ref[step]

    def add_group(g, carry):
        products, where = [], []
        for j in range(GROUP):
            k = g * GROUP + j
            products.append(
                lax.dot_general(
                    tiles_ref[0, k],
                    grad_ref[rows_ref[step, k]],
                    (((0,), (0,)), ((), ())),
                    preferred_element_type=F32,
                )
            )
            where.append(jnp.where(k < count, cols_ref[step, k], col_tiles))
        for j in range(GROUP):
            acc_ref[where[j]] += products[j]
        return carry

    lax.fori_loop(0, (count + GROUP - 1) // GROUP, add_group, 0)
    for i in range(col_tiles):
        out_ref[0, i] = acc_ref[i].astype(out_ref.dtype)


def backward_tiles(tiles, rows, cols, counts, grads, col_tiles):
    sources, slots, tile, _ = tiles.shape
    row_tiles, _, width = grads.shape
    return pl.pallas_call(
        backward_kernel,
        grid_spec=pltpu.PrefetchScalarGridSpec(
            num_scalar_prefetch=3,
            grid=(sources,),
            in_specs=[
                pl.BlockSpec((1, slots, tile, tile), lambda s, *_: (s, 0, 0, 0)),
                pl.BlockSpec((row_tiles, tile, width), lambda s, *_: (0, 0, 0)),
            ],
            out_specs=pl.BlockSpec((1, col_tiles, tile, width), lambda s, *_: (s, 0, 0, 0)),
            scratch_shapes=[pltpu.VMEM((col_tiles + 1, tile, width), F32)],
        ),
        out_shape=jax.ShapeDtypeStruct((sources, col_tiles, tile, width), BF16),
        compiler_params=pltpu.CompilerParams(vmem_limit_bytes=VMEM_LIMIT),
        name="backward_tiles",
    )(rows, cols, counts, tiles, grads)


def copies_of_all(value, axis):
    count = lax.axis_size(axis)
    return lax.all_to_all(jnp.broadcast_to(value[None], (count, *value.shape)), axis, 0, 0)


def sum_over_all(value):
    value = jnp.sum(copies_of_all(value, "rep"), axis=0)
    return jnp.sum(copies_of_all(value, "blk"), axis=0)


def on_device(
    features,
    weight,
    norm_gain,
    norm_shift,
    tile_values,
    tile_rows,
    tile_cols,
    tile_counts,
    cotangent,
):
    tiles, rows, cols, counts = tile_values[0], tile_rows[0], tile_cols[0], tile_counts[0]
    local_rows, width = features.shape
    tile = tiles.shape[-1]
    col_tiles = local_rows // tile
    blk_count = lax.axis_size("blk")
    rep_count = lax.axis_size("rep")
    row_tiles = col_tiles * rep_count
    node_count = local_rows * blk_count * rep_count

    proj = jnp.dot(features, weight, preferred_element_type=F32).astype(BF16)
    gathered = lax.all_gather(proj.reshape(1, col_tiles, tile, width), "blk", axis=0, tiled=True)
    partial_sums, offset = forward_tiles(tiles, rows, cols, counts, gathered, row_tiles)
    parts = lax.all_to_all(partial_sums.reshape(rep_count, local_rows, width), "rep", 0, 0)
    shifted = jnp.sum(parts.astype(F32), axis=0)
    own_mean = jnp.sum(shifted, axis=0) / local_rows
    own_square = jnp.sum((shifted - own_mean) ** 2, axis=0)
    group = copies_of_all(jnp.stack([own_mean, own_square, offset[0]]), "rep")
    group_mean = jnp.sum(group[:, 0], axis=0) / rep_count
    group_square = jnp.sum(group[:, 1], axis=0) + local_rows * jnp.sum(
        (group[:, 0] - group_mean) ** 2, axis=0
    )
    group_offset = jnp.sum(group[:, 2], axis=0)
    everyone = copies_of_all(jnp.stack([group_mean + group_offset, group_square]), "blk")
    feat_mean = jnp.sum(everyone[:, 0], axis=0) / blk_count
    square_sum = jnp.sum(everyone[:, 1], axis=0) + local_rows * rep_count * jnp.sum(
        (everyone[:, 0] - feat_mean) ** 2, axis=0
    )
    inv_std = lax.rsqrt(square_sum / node_count + norm_eps)
    normed = (shifted + (group_offset - feat_mean)) * inv_std
    affine = norm_gain * normed + norm_shift
    gate_value = jax.nn.sigmoid(affine)
    output = (affine * gate_value).astype(BF16)
    grad_affine = cotangent.astype(F32) * gate_value * (1.0 + affine * (1.0 - gate_value))
    grad_beta, grad_gamma = sum_over_all(
        jnp.stack([jnp.sum(grad_affine, axis=0), jnp.sum(grad_affine * normed, axis=0)])
    )
    grad_summed = (
        norm_gain
        * inv_std
        * (grad_affine - grad_beta / node_count - normed * grad_gamma / node_count)
    ).astype(BF16)
    group_grads = lax.all_gather(
        grad_summed.reshape(col_tiles, tile, width), "rep", axis=0, tiled=True
    )
    products = backward_tiles(tiles, rows, cols, counts, group_grads, col_tiles)

    core = lax.axis_index("blk") % 2
    by_core = products.reshape(blk_count // 2, 2, local_rows, width)
    kept = lax.dynamic_index_in_dim(by_core, core, 1, keepdims=False)
    given = lax.dynamic_index_in_dim(by_core, 1 - core, 1, keepdims=False)
    taken = lax.ppermute(given, "blk", [(i, i ^ 1) for i in range(blk_count)])
    chip_sums = (kept.astype(F32) + taken.astype(F32)).astype(BF16)
    same_core = [list(range(c, blk_count, 2)) for c in range(2)]
    terms = lax.all_to_all(chip_sums, "blk", 0, 0, axis_index_groups=same_core)
    proj_grad = jnp.sum(terms.astype(F32), axis=0).astype(BF16)

    grad_x = lax.dot_general(
        proj_grad, weight, (((1,), (1,)), ((), ())), preferred_element_type=F32
    ).astype(BF16)
    weight_term = lax.dot_general(
        features, proj_grad, (((0,), (0,)), ((), ())), preferred_element_type=F32
    )
    pieces = lax.all_to_all(weight_term.reshape(blk_count, -1, width), "blk", 0, 0)
    piece = jnp.sum(copies_of_all(jnp.sum(pieces, axis=0), "rep"), axis=0)
    grad_w = copies_of_all(piece, "blk").reshape(weight.shape)
    return (output, grad_x, grad_w, grad_gamma, grad_beta)


def solution(mesh):
    return jax.shard_map(
        on_device,
        mesh=mesh,
        in_specs=(
            P(("blk", "rep"), None),
            P(),
            P(),
            P(),
            P("blk", "rep", None, None, None),
            P("blk", "rep", None),
            P("blk", "rep", None),
            P("blk", "rep"),
            P(("blk", "rep"), None),
        ),
        out_specs=(P(("blk", "rep"), None), P(("blk", "rep"), None), P(), P(), P()),
        check_vma=False,
    )
```

```python
import functools

import jax
import jax.numpy as jnp
from jax import lax
from jax.experimental import pallas as pl
from jax.experimental.pallas import tpu as pltpu
from jax.sharding import PartitionSpec as P

norm_eps = 1e-05
GROUP = 8
BF16, F32 = jnp.bfloat16, jnp.float32
VMEM_LIMIT = 56 * 2**20
RING = 4
PLACES = ((2, 1), (1, 1), (-1, 1), (2, 0), (0, 1), (1, 0), (-1, 0), (0, 0))
CUTS = (0, 3, 6, 8)
ANY = pl.BlockSpec(memory_space=pl.ANY)
VMEM = pl.BlockSpec(memory_space=pltpu.VMEM)
SMEM = pl.BlockSpec(memory_space=pltpu.SMEM)


def blk_index(z, y, core):
    return (z % RING) * 4 + (y % 2) * 2 + core % 2


def rep_index(x, y):
    return (y % 2) * RING + x % RING


def blk_links():
    spots = [(z, y, c) for z in range(RING) for y in range(2) for c in range(2)]

    def link(dz, dy, dc):
        pairs = [(blk_index(z, y, c), blk_index(z + dz, y + dy, c + dc)) for z, y, c in spots]
        return lambda value: lax.ppermute(value, "blk", pairs)

    return link(1, 0, 0), link(-1, 0, 0), link(0, 1, 0), link(0, 0, 1)


def rep_links():
    spots = [(x, y) for x in range(RING) for y in range(2)]

    def link(dx, dy):
        pairs = [(rep_index(x, y), rep_index(x + dx, y + dy)) for x, y in spots]
        return lambda value: lax.ppermute(value, "rep", pairs)

    return link(1, 0), link(-1, 0), link(0, 1)


def gather_tree(own, up, down, pair):
    below, above, beside = up(own), down(own), pair(own)
    below_beside, above_beside, far = pair(below), down(beside), up(below)
    a, b, c, _ = CUTS[1], CUTS[2], CUTS[3], None
    far_beside = [(0, pair(far[:a])), (a, down(above_beside[a:b])), (b, up(below_beside[b:c]))]
    whole = {
        (0, 0): own,
        (-1, 0): below,
        (1, 0): above,
        (0, 1): beside,
        (-1, 1): below_beside,
        (1, 1): above_beside,
        (2, 0): far,
    }
    return [far_beside if place == (2, 1) else [(0, whole[place])] for place in PLACES]


def placed(part, first, like):
    after = like.shape[0] - first - part.shape[0]
    return jnp.pad(part.astype(F32), ((first, after), (0, 0), (0, 0)))


def scatter_tree(blocks, up, down, pair):
    wide = {place: block.astype(F32) for place, block in blocks.items()}
    sent = {place: block.astype(BF16) for place, block in blocks.items()}
    a, b = CUTS[1], CUTS[2]
    corner = sent[2, 1]
    far = wide[2, 0] + placed(pair(corner[:a]), 0, corner)
    above_beside = wide[1, 1] + placed(up(corner[a:b]), a, corner)
    below_beside = wide[-1, 1] + placed(down(corner[b:]), b, corner)
    below = (
        wide[-1, 0] + pair(below_beside.astype(BF16)).astype(F32) + down(far.astype(BF16)).astype(F32)
    )
    beside = wide[0, 1] + up(above_beside.astype(BF16)).astype(F32)
    return (
        wide[0, 0]
        + up(sent[1, 0]).astype(F32)
        + down(below.astype(BF16)).astype(F32)
        + pair(beside.astype(BF16)).astype(F32)
    )


def forward_kernel(layout, order_ref, dest_ref, rows_ref, cols_ref, counts_ref, tiles_ref, *refs):
    sources, row_groups = len(layout), len(PLACES)
    parts = sum(len(firsts) for firsts in layout)
    shard_refs, refs = refs[:parts], refs[parts:]
    out_refs, offset_ref = refs[:row_groups], refs[row_groups]
    tiles_v, shards_v, acc_ref, tile_sem, part_sem = refs[row_groups + 1 :]
    col_tiles = out_refs[0].shape[0]
    row_tiles = row_groups * col_tiles

    copies, part = [], 0
    for i, firsts in enumerate(layout):
        source = order_ref[i]
        own = [pltpu.make_async_copy(tiles_ref.at[source], tiles_v.at[i], tile_sem.at[i])]
        for first in firsts:
            size = shard_refs[part].shape[0]
            own.append(
                pltpu.make_async_copy(
                    shard_refs[part], shards_v.at[i, pl.ds(first, size)], part_sem.at[part]
                )
            )
            part += 1
        for copy in own:
            copy.start()
        copies.append(own)

    def zero(i, carry):
        acc_ref[i] = jnp.zeros(acc_ref.shape[1:], F32)
        return carry

    lax.fori_loop(0, row_tiles + 1, zero, 0)

    for i in range(sources):
        for copy in copies[i]:
            copy.wait()
        source = order_ref[i]
        count = counts_ref[source]

        def add_group(g, carry, i=i, source=source, count=count):
            products, where = [], []
            for j in range(GROUP):
                k = g * GROUP + j
                products.append(
                    jnp.dot(tiles_v[i, k], shards_v[i, cols_ref[source, k]], preferred_element_type=F32)
                )
                where.append(jnp.where(k < count, rows_ref[source, k], row_tiles))
            for j in range(GROUP):
                acc_ref[where[j]] += products[j]
            return carry

        lax.fori_loop(0, (count + GROUP - 1) // GROUP, add_group, 0)

    def total(i, carry):
        return carry + jnp.sum(acc_ref[i].reshape(-1, 8, acc_ref.shape[2]), axis=0)

    sums = lax.fori_loop(0, row_tiles, total, jnp.zeros((8, acc_ref.shape[2]), F32))
    offset = jnp.sum(sums, axis=0, keepdims=True) / (row_tiles * acc_ref.shape[1])
    offset_ref[...] = offset
    for d in range(row_groups):
        base = dest_ref[d] * col_tiles

        def put(i, carry, d=d, base=base):
            out_refs[d][i] = (acc_ref[base + i] - offset).astype(BF16)
            return carry

        lax.fori_loop(0, col_tiles, put, 0)


def forward_tiles(order, dests, rows, cols, counts, tiles, shards):
    arrays = [array for parts in shards for _, array in parts]
    layout = tuple(tuple(first for first, _ in parts) for parts in shards)
    sources, slots, tile, _ = tiles.shape
    col_tiles, width = CUTS[-1], arrays[0].shape[2]
    row_tiles = col_tiles * len(PLACES)
    return pl.pallas_call(
        functools.partial(forward_kernel, layout),
        in_specs=[SMEM] * 5 + [ANY] * (1 + len(arrays)),
        out_specs=[VMEM] * (len(PLACES) + 1),
        out_shape=[jax.ShapeDtypeStruct((col_tiles, tile, width), BF16)] * len(PLACES)
        + [jax.ShapeDtypeStruct((1, width), F32)],
        scratch_shapes=[
            pltpu.VMEM((sources, slots, tile, tile), BF16),
            pltpu.VMEM((sources, col_tiles, tile, width), BF16),
            pltpu.VMEM((row_tiles + 1, tile, width), F32),
            pltpu.SemaphoreType.DMA((sources,)),
            pltpu.SemaphoreType.DMA((len(arrays),)),
        ],
        compiler_params=pltpu.CompilerParams(vmem_limit_bytes=VMEM_LIMIT),
        cost_estimate=pl.CostEstimate(flops=6 * 10**9, bytes_accessed=30 * 2**20, transcendentals=0),
        name="forward_tiles",
    )(order, dests, rows, cols, counts, tiles, *arrays)


def backward_kernel(layout, split, order_ref, dest_ref, rows_ref, cols_ref, counts_ref, tiles_ref, *refs):
    parts = sum(len(firsts) for firsts in layout)
    grad_refs, refs = refs[:parts], refs[parts:]
    out_refs, (tiles_v, grads_v, acc_ref, tile_sem, part_sem) = refs[: len(split)], refs[len(split) :]
    sources = sum(split)
    col_tiles = out_refs[0].shape[1]

    copies, part = [], 0
    for i, firsts in enumerate(layout):
        base = dest_ref[i] * col_tiles
        for first in firsts:
            size = grad_refs[part].shape[0]
            copies.append(
                pltpu.make_async_copy(
                    grad_refs[part], grads_v.at[pl.ds(base + first, size)], part_sem.at[part]
                )
            )
            part += 1
    tile_copies = [
        pltpu.make_async_copy(tiles_ref.at[order_ref[i]], tiles_v.at[i], tile_sem.at[i])
        for i in range(sources)
    ]
    for copy in copies + tile_copies:
        copy.start()
    for copy in copies:
        copy.wait()

    spots = [(n, m) for n, size in enumerate(split) for m in range(size)]
    for i in range(sources):
        for t in range(col_tiles + 1):
            acc_ref[t] = jnp.zeros(acc_ref.shape[1:], F32)
        tile_copies[i].wait()
        source = order_ref[i]
        count = counts_ref[source]

        def add_group(g, carry, i=i, source=source, count=count):
            products, where = [], []
            for j in range(GROUP):
                k = g * GROUP + j
                products.append(
                    lax.dot_general(
                        tiles_v[i, k],
                        grads_v[rows_ref[source, k]],
                        (((0,), (0,)), ((), ())),
                        preferred_element_type=F32,
                    )
                )
                where.append(jnp.where(k < count, cols_ref[source, k], col_tiles))
            for j in range(GROUP):
                acc_ref[where[j]] += products[j]
            return carry

        lax.fori_loop(0, (count + GROUP - 1) // GROUP, add_group, 0)
        n, m = spots[i]
        for t in range(col_tiles):
            out_refs[n][m, t] = acc_ref[t].astype(BF16)


def backward_tiles(split, order, dests, rows, cols, counts, tiles, grads):
    arrays = [array for parts in grads for _, array in parts]
    layout = tuple(tuple(first for first, _ in parts) for parts in grads)
    _, slots, tile, _ = tiles.shape
    sources = sum(split)
    col_tiles, width = CUTS[-1], arrays[0].shape[2]
    return pl.pallas_call(
        functools.partial(backward_kernel, layout, split),
        in_specs=[SMEM] * 5 + [ANY] * (1 + len(arrays)),
        out_specs=[VMEM] * len(split),
        out_shape=[jax.ShapeDtypeStruct((n, col_tiles, tile, width), BF16) for n in split],
        scratch_shapes=[
            pltpu.VMEM((sources, slots, tile, tile), BF16),
            pltpu.VMEM((col_tiles * len(PLACES), tile, width), BF16),
            pltpu.VMEM((col_tiles + 1, tile, width), F32),
            pltpu.SemaphoreType.DMA((sources,)),
            pltpu.SemaphoreType.DMA((len(arrays),)),
        ],
        compiler_params=pltpu.CompilerParams(vmem_limit_bytes=VMEM_LIMIT),
        cost_estimate=pl.CostEstimate(flops=3 * 10**9, bytes_accessed=20 * 2**20, transcendentals=0),
        name="backward_tiles",
    )(order, dests, rows, cols, counts, tiles, *arrays)


def copies_of_all(value, axis):
    count = lax.axis_size(axis)
    return lax.all_to_all(jnp.broadcast_to(value[None], (count, *value.shape)), axis, 0, 0)


def sum_over_all(value):
    value = jnp.sum(copies_of_all(value, "rep"), axis=0)
    return jnp.sum(copies_of_all(value, "blk"), axis=0)


def on_device(
    features,
    weight,
    norm_gain,
    norm_shift,
    tile_values,
    tile_rows,
    tile_cols,
    tile_counts,
    cotangent,
):
    tiles, rows, cols, counts = tile_values[0], tile_rows[0], tile_cols[0], tile_counts[0]
    local_rows, width = features.shape
    tile = tiles.shape[-1]
    col_tiles = local_rows // tile
    blk_count = lax.axis_size("blk")
    rep_count = lax.axis_size("rep")
    node_count = local_rows * blk_count * rep_count
    blk, rep = lax.axis_index("blk"), lax.axis_index("rep")
    z, y_low, core = blk // 4, (blk // 2) % 2, blk % 2
    y_high, x = rep // RING, rep % RING
    own_core = jnp.stack([blk_index(z + a + RING, y_low + b, core) for a, b in PLACES])
    other_core = own_core + (1 - 2 * core)
    dests = jnp.stack([rep_index(x + a + RING, y_high + b) for a, b in PLACES])
    *blk_tree, across = blk_links()
    rep_tree = rep_links()

    mine = gather_tree(features.reshape(col_tiles, tile, width), *blk_tree)
    theirs = [[(first, across(array)) for first, array in parts] for parts in mine]
    backwards = slice(None, None, -1)
    *blocks, offset = forward_tiles(
        jnp.stack([own_core[backwards], other_core[backwards]], axis=1).reshape(-1),
        dests,
        rows,
        cols,
        counts,
        tiles,
        [parts for both in zip(mine[backwards], theirs[backwards]) for parts in both],
    )
    shifted = scatter_tree(dict(zip(PLACES, blocks)), *rep_tree).reshape(local_rows, width)
    aggregate = shifted.astype(BF16)
    projected = jnp.dot(aggregate, weight, preferred_element_type=F32)
    own_mean = jnp.sum(projected, axis=0) / local_rows
    own_square = jnp.sum((projected - own_mean) ** 2, axis=0)
    moved = jnp.dot(offset, weight.astype(F32), precision=lax.Precision.HIGHEST)
    group = copies_of_all(jnp.stack([own_mean, own_square, moved[0], offset[0]]), "rep")
    group_mean = jnp.sum(group[:, 0], axis=0) / rep_count
    group_square = jnp.sum(group[:, 1], axis=0) + local_rows * jnp.sum(
        (group[:, 0] - group_mean) ** 2, axis=0
    )
    group_moved = jnp.sum(group[:, 2], axis=0)
    group_offset = jnp.sum(group[:, 3], axis=0)
    everyone = copies_of_all(jnp.stack([group_mean + group_moved, group_square]), "blk")
    feat_mean = jnp.sum(everyone[:, 0], axis=0) / blk_count
    square_sum = jnp.sum(everyone[:, 1], axis=0) + local_rows * rep_count * jnp.sum(
        (everyone[:, 0] - feat_mean) ** 2, axis=0
    )
    inv_std = lax.rsqrt(square_sum / node_count + norm_eps)
    normed = (projected + (group_moved - feat_mean)) * inv_std
    affine = norm_gain * normed + norm_shift
    gate_value = jax.nn.sigmoid(affine)
    output = (affine * gate_value).astype(BF16)
    grad_affine = cotangent.astype(F32) * gate_value * (1.0 + affine * (1.0 - gate_value))
    grad_beta, grad_gamma = sum_over_all(
        jnp.stack([jnp.sum(grad_affine, axis=0), jnp.sum(grad_affine * normed, axis=0)])
    )
    grad_summed = (
        norm_gain
        * inv_std
        * (grad_affine - grad_beta / node_count - normed * grad_gamma / node_count)
    ).astype(BF16)

    sent = lax.dot_general(
        grad_summed, weight, (((1,), (1,)), ((), ())), preferred_element_type=F32
    ).astype(BF16)
    grads = gather_tree(sent.reshape(col_tiles, tile, width), *rep_tree)
    products = {}
    for low, high, cuts in ((0, 4, (1, 3)), (4, 8, (4,))):
        order = jnp.concatenate([other_core[low:high], own_core[low:high]])
        given_kept = backward_tiles(
            (*cuts, high - low), order, dests, rows, cols, counts, tiles, grads
        )
        kept, given = given_kept[-1], given_kept[:-1]
        taken = [(array, n) for block in given for array in [across(block)] for n in range(block.shape[0])]
        for i, place in enumerate(PLACES[low:high]):
            array, n = taken[i]
            products[place] = kept[i].astype(F32) + array[n].astype(F32)
    grad_x = scatter_tree(products, *blk_tree).astype(BF16).reshape(local_rows, width)

    weight_term = lax.dot_general(
        aggregate, grad_summed, (((0,), (0,)), ((), ())), preferred_element_type=F32
    ) + group_offset[:, None] * jnp.sum(grad_summed.astype(F32), axis=0)
    pieces = lax.all_to_all(weight_term.reshape(blk_count, -1, width), "blk", 0, 0)
    piece = jnp.sum(copies_of_all(jnp.sum(pieces, axis=0), "rep"), axis=0)
    grad_w = copies_of_all(piece, "blk").reshape(weight.shape)
    return (output, grad_x, grad_w, grad_gamma, grad_beta)


def solution(mesh):
    return jax.shard_map(
        on_device,
        mesh=mesh,
        in_specs=(
            P(("blk", "rep"), None),
            P(),
            P(),
            P(),
            P("blk", "rep", None, None, None),
            P("blk", "rep", None),
            P("blk", "rep", None),
            P("blk", "rep"),
            P(("blk", "rep"), None),
        ),
        out_specs=(P(("blk", "rep"), None), P(("blk", "rep"), None), P(), P(), P()),
        check_vma=False,
    )
```

```python
import functools

import jax
import jax.numpy as jnp
from jax import lax
from jax.experimental import pallas as pl
from jax.experimental.pallas import tpu as pltpu
from jax.sharding import PartitionSpec as P

norm_eps = 1e-05
GROUP = 16
BF16, F32 = jnp.bfloat16, jnp.float32
VMEM_LIMIT = 56 * 2**20
RING = 4
PLACES = ((2, 1), (1, 1), (-1, 1), (2, 0), (0, 1), (1, 0), (-1, 0), (0, 0))
ANY = pl.BlockSpec(memory_space=pl.ANY)
VMEM = pl.BlockSpec(memory_space=pltpu.VMEM)
SMEM = pl.BlockSpec(memory_space=pltpu.SMEM)


def blk_index(z, y, core):
    return (z % RING) * 4 + (y % 2) * 2 + core % 2


def rep_index(x, y):
    return (y % 2) * RING + x % RING


def blk_links():
    spots = [(z, y, c) for z in range(RING) for y in range(2) for c in range(2)]

    def link(dz, dy, dc):
        pairs = [(blk_index(z, y, c), blk_index(z + dz, y + dy, c + dc)) for z, y, c in spots]
        return lambda value: lax.ppermute(value, "blk", pairs)

    return link(1, 0, 0), link(-1, 0, 0), link(0, 1, 0), link(0, 0, 1)


def rep_links():
    spots = [(x, y) for x in range(RING) for y in range(2)]

    def link(dx, dy):
        pairs = [(rep_index(x, y), rep_index(x + dx, y + dy)) for x, y in spots]
        return lambda value: lax.ppermute(value, "rep", pairs)

    return link(1, 0), link(-1, 0), link(0, 1)


def gather_tree(own, up, down, pair):
    half = own.shape[0] // 2
    below, above, beside = up(own), down(own), pair(own)
    below_beside, above_beside, far = pair(below), down(beside), up(below)
    far_beside = [(0, down(above_beside[:half])), (half, up(below_beside[half:]))]
    whole = {
        (0, 0): own,
        (-1, 0): below,
        (1, 0): above,
        (0, 1): beside,
        (-1, 1): below_beside,
        (1, 1): above_beside,
        (2, 0): far,
    }
    return [far_beside if place == (2, 1) else [(0, whole[place])] for place in PLACES]


def scatter_first(corner, blocks, up, down):
    low, high = corner
    half = low.shape[0]
    none = ((0, 0), (0, 0))
    above_beside = blocks[1, 1].astype(F32) + jnp.pad(
        up(low.astype(BF16)).astype(F32), ((0, half), *none)
    )
    below_beside = blocks[-1, 1].astype(F32) + jnp.pad(
        down(high.astype(BF16)).astype(F32), ((half, 0), *none)
    )
    return above_beside.astype(BF16), below_beside.astype(BF16), blocks[2, 0].astype(BF16)


def scatter_second(leaving, blocks, up, down, pair):
    above_beside, below_beside, far = leaving
    below = blocks[-1, 0].astype(F32) + pair(below_beside).astype(F32) + down(far).astype(F32)
    beside = blocks[0, 1].astype(F32) + up(above_beside).astype(F32)
    return below.astype(BF16), beside.astype(BF16), blocks[1, 0].astype(BF16)


def scatter_third(leaving, own, up, down, pair):
    below, beside, above = leaving
    return (
        own.astype(F32)
        + up(above).astype(F32)
        + down(below).astype(F32)
        + pair(beside).astype(F32)
    )


def run_list(first, last, spare, tile_list, panel_list, key_list, multiply, acc_ref):
    def add_group(g, carry):
        products = [
            multiply(tile_list[g * GROUP + j], panel_list[g * GROUP + j]) for j in range(GROUP)
        ]
        for j in range(GROUP):
            acc_ref[key_list[g * GROUP + j]] += products[j]
        return carry

    lax.fori_loop(first, last, add_group, 0)


def zero_all(acc_ref):
    def zero(i, carry):
        acc_ref[i] = jnp.zeros(acc_ref.shape[1:], F32)
        return carry

    lax.fori_loop(0, acc_ref.shape[0], zero, 0)


def fill_tail(count, spare, tile_list, panel_list, key_list):
    for j in range(GROUP):
        tile_list[count + j] = 0
        panel_list[count + j] = 0
        key_list[count + j] = spare


def forward_kernel(layout, low, high, waits, order_ref, dest_ref, rows_ref, cols_ref, counts_ref, tiles_ref, *refs):
    first_call = low == 0
    sources = len(layout)
    slots = rows_ref.shape[1]
    parts = sum(len(firsts) for firsts in layout)
    shard_refs, refs = refs[:parts], refs[parts + waits :]
    if not first_call:
        given_offset_ref, refs = refs[0], refs[1:]
    places = high - low
    outs = places + 2 * first_call
    out_refs, refs = refs[:outs], refs[outs:]
    tiles_v, shards_v, acc_ref, tile_list, panel_list, key_list, place_of, tile_sem, part_sem = refs
    col_tiles = out_refs[-2].shape[0]
    row_tiles = places * col_tiles

    copies, part = [], 0
    for i, firsts in enumerate(layout):
        own = [
            pltpu.make_async_copy(
                tiles_ref.at[order_ref[i]], tiles_v.at[pl.ds(i * slots, slots)], tile_sem.at[i]
            )
        ]
        for first in firsts:
            size = shard_refs[part].shape[0]
            own.append(
                pltpu.make_async_copy(
                    shard_refs[part],
                    shards_v.at[pl.ds(i * col_tiles + first, size)],
                    part_sem.at[part],
                )
            )
            part += 1
        for copy in own:
            copy.start()
        copies.append(own)

    zero_all(acc_ref)
    for d in range(len(PLACES)):
        place_of[dest_ref[d]] = d - low
    count, ends = jnp.int32(0), []
    for i in range(sources):
        source = order_ref[i]

        def enlist(k, count, i=i, source=source):
            row = rows_ref[source, k]
            place = place_of[row // col_tiles]
            tile_list[count] = i * slots + k
            panel_list[count] = i * col_tiles + cols_ref[source, k]
            key_list[count] = place * col_tiles + row % col_tiles
            return count + jnp.where((place >= 0) & (place < places), 1, 0)

        count = lax.fori_loop(0, counts_ref[source], enlist, count)
        ends.append(count)
    fill_tail(count, row_tiles, tile_list, panel_list, key_list)

    def multiply(tile, panel):
        return jnp.dot(tiles_v[tile], shards_v[panel], preferred_element_type=F32)

    lists = (row_tiles, tile_list, panel_list, key_list, multiply, acc_ref)
    for own in copies[: sources // 2]:
        for copy in own:
            copy.wait()
    middle = ends[sources // 2 - 1] // GROUP
    run_list(0, middle, *lists)
    for own in copies[sources // 2 :]:
        for copy in own:
            copy.wait()
    run_list(middle, (count + GROUP - 1) // GROUP, *lists)

    if first_call:

        def total(i, carry):
            return carry + jnp.sum(acc_ref[i].reshape(-1, 8, acc_ref.shape[2]), axis=0)

        sums = lax.fori_loop(0, row_tiles, total, jnp.zeros((8, acc_ref.shape[2]), F32))
        offset = jnp.sum(sums, axis=0, keepdims=True) / (row_tiles * acc_ref.shape[1])
        out_refs[-1][...] = offset
        half = col_tiles // 2
        spans = [(out_refs[0], 0, half), (out_refs[1], half, half)]
        spans += [(out_refs[d + 1], d * col_tiles, col_tiles) for d in range(1, places)]
    else:
        offset = given_offset_ref[...]
        spans = [(out_refs[d], d * col_tiles, col_tiles) for d in range(places)]
    for out_ref, base, size in spans:

        def put(i, carry, out_ref=out_ref, base=base):
            out_ref[i] = (acc_ref[base + i] - offset).astype(BF16)
            return carry

        lax.fori_loop(0, size, put, 0)


def forward_tiles(low, high, order, dests, rows, cols, counts, tiles, shards, offset=None, after=()):
    arrays = [array for parts in shards for _, array in parts]
    layout = tuple(tuple(first for first, _ in parts) for parts in shards)
    sources, slots, tile, _ = tiles.shape
    width = arrays[0].shape[2]
    col_tiles = arrays[0].shape[0]
    places = high - low
    cap = sources * slots + GROUP
    sizes = [col_tiles] * places
    out_shape = [jax.ShapeDtypeStruct((size, tile, width), BF16) for size in sizes]
    if low == 0:
        halves = [jax.ShapeDtypeStruct((col_tiles // 2, tile, width), BF16)] * 2
        out_shape = halves + out_shape[1:] + [jax.ShapeDtypeStruct((1, width), F32)]
    given = [] if low == 0 else [offset]
    return pl.pallas_call(
        functools.partial(forward_kernel, layout, low, high, len(after)),
        in_specs=[SMEM] * 5 + [ANY] * (1 + len(arrays) + len(after)) + [VMEM] * len(given),
        out_specs=[VMEM] * len(out_shape),
        out_shape=out_shape,
        scratch_shapes=[
            pltpu.VMEM((sources * slots, tile, tile), BF16),
            pltpu.VMEM((sources * col_tiles, tile, width), BF16),
            pltpu.VMEM((places * col_tiles + 1, tile, width), F32),
            pltpu.SMEM((cap,), jnp.int32),
            pltpu.SMEM((cap,), jnp.int32),
            pltpu.SMEM((cap,), jnp.int32),
            pltpu.SMEM((len(PLACES),), jnp.int32),
            pltpu.SemaphoreType.DMA((sources,)),
            pltpu.SemaphoreType.DMA((len(arrays),)),
        ],
        compiler_params=pltpu.CompilerParams(vmem_limit_bytes=VMEM_LIMIT),
        cost_estimate=pl.CostEstimate(flops=3 * 10**9, bytes_accessed=30 * 2**20, transcendentals=0),
        name="forward_tiles",
    )(order, dests, rows, cols, counts, tiles, *arrays, *after, *given)


def backward_kernel(layout, split, waits, order_ref, dest_ref, rows_ref, cols_ref, counts_ref, tiles_ref, *refs):
    parts = sum(len(firsts) for firsts in layout)
    grad_refs, refs = refs[:parts], refs[parts + waits :]
    out_refs, refs = refs[: len(split)], refs[len(split) :]
    tiles_v, grads_v, acc_ref, tile_list, panel_list, key_list, tile_sem, part_sem = refs
    sources = sum(split)
    slots = rows_ref.shape[1]
    col_tiles = out_refs[0].shape[1]

    copies, part = [], 0
    for i, firsts in enumerate(layout):
        base = dest_ref[i] * col_tiles
        for first in firsts:
            size = grad_refs[part].shape[0]
            copies.append(
                pltpu.make_async_copy(
                    grad_refs[part], grads_v.at[pl.ds(base + first, size)], part_sem.at[part]
                )
            )
            part += 1
    tile_copies = [
        pltpu.make_async_copy(
            tiles_ref.at[order_ref[i]], tiles_v.at[pl.ds(i * slots, slots)], tile_sem.at[i]
        )
        for i in range(sources)
    ]
    for copy in copies + tile_copies:
        copy.start()

    zero_all(acc_ref)
    count, ends = jnp.int32(0), []
    for i in range(sources):
        source = order_ref[i]

        def enlist(k, count, i=i, source=source):
            tile_list[count] = i * slots + k
            panel_list[count] = rows_ref[source, k]
            key_list[count] = i * col_tiles + cols_ref[source, k]
            return count + 1

        count = lax.fori_loop(0, counts_ref[source], enlist, count)
        ends.append(count)
    fill_tail(count, sources * col_tiles, tile_list, panel_list, key_list)

    def multiply(tile, panel):
        return lax.dot_general(
            tiles_v[tile], grads_v[panel], (((0,), (0,)), ((), ())), preferred_element_type=F32
        )

    lists = (sources * col_tiles, tile_list, panel_list, key_list, multiply, acc_ref)
    for copy in copies + tile_copies[: sources // 2]:
        copy.wait()
    middle = ends[sources // 2 - 1] // GROUP
    run_list(0, middle, *lists)
    for copy in tile_copies[sources // 2 :]:
        copy.wait()
    run_list(middle, (count + GROUP - 1) // GROUP, *lists)

    first = 0
    for n, size in enumerate(split):
        for m in range(size):

            def put(t, carry, n=n, m=m, base=(first + m) * col_tiles):
                out_refs[n][m, t] = acc_ref[base + t].astype(BF16)
                return carry

            lax.fori_loop(0, col_tiles, put, 0)
        first += size


def backward_tiles(split, order, dests, rows, cols, counts, tiles, grads, after=()):
    arrays = [array for parts in grads for _, array in parts]
    layout = tuple(tuple(first for first, _ in parts) for parts in grads)
    _, slots, tile, _ = tiles.shape
    sources = sum(split)
    width = arrays[0].shape[2]
    row_tiles = sum(array.shape[0] for array in arrays)
    col_tiles = row_tiles // len(PLACES)
    cap = sources * slots + GROUP
    return pl.pallas_call(
        functools.partial(backward_kernel, layout, split, len(after)),
        in_specs=[SMEM] * 5 + [ANY] * (1 + len(arrays) + len(after)),
        out_specs=[VMEM] * len(split),
        out_shape=[jax.ShapeDtypeStruct((n, col_tiles, tile, width), BF16) for n in split],
        scratch_shapes=[
            pltpu.VMEM((sources * slots, tile, tile), BF16),
            pltpu.VMEM((row_tiles, tile, width), BF16),
            pltpu.VMEM((sources * col_tiles + 1, tile, width), F32),
            pltpu.SMEM((cap,), jnp.int32),
            pltpu.SMEM((cap,), jnp.int32),
            pltpu.SMEM((cap,), jnp.int32),
            pltpu.SemaphoreType.DMA((sources,)),
            pltpu.SemaphoreType.DMA((len(arrays),)),
        ],
        compiler_params=pltpu.CompilerParams(vmem_limit_bytes=VMEM_LIMIT),
        cost_estimate=pl.CostEstimate(flops=3 * 10**9, bytes_accessed=20 * 2**20, transcendentals=0),
        name="backward_tiles",
    )(order, dests, rows, cols, counts, tiles, *arrays, *after)


def sum_first_kernel(value_ref, *refs):
    refs[-1][...] = jnp.sum(value_ref[...], axis=0)


def sum_first(value, after):
    return pl.pallas_call(
        sum_first_kernel,
        in_specs=[VMEM] + [ANY] * len(after),
        out_specs=VMEM,
        out_shape=jax.ShapeDtypeStruct(value.shape[1:], value.dtype),
        name="sum_first",
    )(value, *after)


def weight_kernel(aggregate_ref, grad_ref, offset_ref, *refs):
    grads = grad_ref[...]
    sums = jnp.sum(grads.astype(F32), axis=0, keepdims=True)
    refs[-1][...] = (
        lax.dot_general(
            aggregate_ref[...], grads, (((0,), (0,)), ((), ())), preferred_element_type=F32
        )
        + offset_ref[...] * sums
    )


def weight_terms(aggregate, grads, offset, after):
    width = grads.shape[1]
    return pl.pallas_call(
        weight_kernel,
        in_specs=[VMEM] * 3 + [ANY] * len(after),
        out_specs=VMEM,
        out_shape=jax.ShapeDtypeStruct((width, width), F32),
        name="weight_terms",
    )(aggregate, grads, jnp.broadcast_to(offset[:, None], (width, width)), *after)


def copies_of_all(value, axis):
    count = lax.axis_size(axis)
    return lax.all_to_all(jnp.broadcast_to(value[None], (count, *value.shape)), axis, 0, 0)


def on_device(
    features,
    weight,
    norm_gain,
    norm_shift,
    tile_values,
    tile_rows,
    tile_cols,
    tile_counts,
    cotangent,
):
    tiles, rows, cols, counts = tile_values[0], tile_rows[0], tile_cols[0], tile_counts[0]
    local_rows, width = features.shape
    tile = tiles.shape[-1]
    col_tiles = local_rows // tile
    blk_count = lax.axis_size("blk")
    rep_count = lax.axis_size("rep")
    node_count = local_rows * blk_count * rep_count
    blk, rep = lax.axis_index("blk"), lax.axis_index("rep")
    z, y_low, core = blk // 4, (blk // 2) % 2, blk % 2
    y_high, x = rep // RING, rep % RING
    own_core = jnp.stack([blk_index(z + a + RING, y_low + b, core) for a, b in PLACES])
    other_core = own_core + (1 - 2 * core)
    dests = jnp.stack([rep_index(x + a + RING, y_high + b) for a, b in PLACES])
    *blk_tree, across = blk_links()
    rep_tree = rep_links()

    mine = gather_tree(features.reshape(col_tiles, tile, width), *blk_tree)
    theirs = [[(first, across(array)) for first, array in parts] for parts in mine]
    backwards = slice(None, None, -1)
    lists = (dests, rows, cols, counts, tiles)
    order = jnp.stack([own_core[backwards], other_core[backwards]], axis=1).reshape(-1)
    shards = [parts for both in zip(mine[backwards], theirs[backwards]) for parts in both]
    up, down, pair = rep_tree
    *corner, above_beside, below_beside, far, offset = forward_tiles(0, 4, order, *lists, shards)
    blocks = {(1, 1): above_beside, (-1, 1): below_beside, (2, 0): far}
    leaving = scatter_first(corner, blocks, up, down)
    blocks.update(
        zip(PLACES[4:], forward_tiles(4, 8, order, *lists, shards, offset, [leaving[0][:1, :16, :128]]))
    )
    leaving = scatter_second(leaving, blocks, *rep_tree)
    shifted = scatter_third(leaving, blocks[0, 0], *rep_tree).reshape(local_rows, width)
    aggregate = shifted.astype(BF16)
    projected = jnp.dot(aggregate, weight, preferred_element_type=F32)
    own_mean = jnp.sum(projected, axis=0) / local_rows
    own_square = jnp.sum((projected - own_mean) ** 2, axis=0)
    moved = jnp.dot(offset, weight.astype(F32), precision=lax.Precision.HIGHEST)
    everyone = copies_of_all(
        jnp.stack([own_mean, own_square, moved[0], offset[0]]), ("blk", "rep")
    ).reshape(blk_count, rep_count, 4, width)
    moves = jnp.sum(everyone[:, :, 2], axis=1)
    means = everyone[:, :, 0] + moves[:, None]
    feat_mean = jnp.sum(means, axis=(0, 1)) / (blk_count * rep_count)
    square_sum = jnp.sum(everyone[:, :, 1], axis=(0, 1)) + local_rows * jnp.sum(
        (means - feat_mean) ** 2, axis=(0, 1)
    )
    group = lax.dynamic_index_in_dim(everyone, blk, 0, keepdims=False)
    group_moved, group_offset = jnp.sum(group[:, 2], axis=0), jnp.sum(group[:, 3], axis=0)
    inv_std = lax.rsqrt(square_sum / node_count + norm_eps)
    normed = (projected + (group_moved - feat_mean)) * inv_std
    affine = norm_gain * normed + norm_shift
    gate_value = jax.nn.sigmoid(affine)
    output = (affine * gate_value).astype(BF16)
    grad_affine = cotangent.astype(F32) * gate_value * (1.0 + affine * (1.0 - gate_value))
    grad_beta, grad_gamma = jnp.sum(
        copies_of_all(
            jnp.stack([jnp.sum(grad_affine, axis=0), jnp.sum(grad_affine * normed, axis=0)]),
            ("blk", "rep"),
        ),
        axis=0,
    )
    grad_summed = (
        norm_gain
        * inv_std
        * (grad_affine - grad_beta / node_count - normed * grad_gamma / node_count)
    ).astype(BF16)

    sent = lax.dot_general(
        grad_summed, weight, (((1,), (1,)), ((), ())), preferred_element_type=F32
    ).astype(BF16)
    grads = gather_tree(sent.reshape(col_tiles, tile, width), *rep_tree)
    arrived = {place: parts[0][1] for place, parts in zip(PLACES, grads)}
    weight_term = weight_terms(
        aggregate, grad_summed, group_offset, [arrived[1, 0]]
    )
    pieces = lax.all_to_all(weight_term.reshape(blk_count, -1, width), "blk", 0, 0)
    piece = sum_first(pieces, [arrived[-1, 1]])
    terms = copies_of_all(piece, "rep")

    def of_chip(low, high, cuts, after):
        order = jnp.concatenate([other_core[low:high], own_core[low:high]])
        *given, kept = backward_tiles((*cuts, high - low), order, *lists, grads, after)
        taken = [block for part in given for block in across(part)]
        return {
            place: kept[i].astype(F32) + taken[i].astype(F32)
            for i, place in enumerate(PLACES[low:high])
        }

    up, down, pair = blk_tree
    products = of_chip(0, 4, (1, 3), [terms])
    half = col_tiles // 2
    corner = products[2, 1]
    leaving = scatter_first((corner[:half], corner[half:]), products, up, down)
    products.update(of_chip(4, 8, (4,), [leaving[0][:1, :16, :128]]))
    leaving = scatter_second(leaving, products, *blk_tree)
    grad_w = copies_of_all(sum_first(terms, [leaving[0][:1, :16, :128]]), "blk").reshape(weight.shape)
    grad_x = scatter_third(leaving, products[0, 0], *blk_tree).astype(BF16)
    return (output, grad_x.reshape(local_rows, width), grad_w, grad_gamma, grad_beta)


def solution(mesh):
    return jax.shard_map(
        on_device,
        mesh=mesh,
        in_specs=(
            P(("blk", "rep"), None),
            P(),
            P(),
            P(),
            P("blk", "rep", None, None, None),
            P("blk", "rep", None),
            P("blk", "rep", None),
            P("blk", "rep"),
            P(("blk", "rep"), None),
        ),
        out_specs=(P(("blk", "rep"), None), P(("blk", "rep"), None), P(), P(), P()),
        check_vma=False,
    )
```

```python
import functools

import jax
import jax.numpy as jnp
from jax import lax
from jax.experimental import pallas as pl
from jax.experimental.pallas import tpu as pltpu
from jax.sharding import PartitionSpec as P

norm_eps = 1e-05
GROUP = 32
BF16, F32 = jnp.bfloat16, jnp.float32
RING = 4
PLACES = ((2, 1), (1, 1), (-1, 1), (2, 0), (0, 1), (1, 0), (-1, 0), (0, 0))
ANY = pl.BlockSpec(memory_space=pl.ANY)
VMEM = pl.BlockSpec(memory_space=pltpu.VMEM)
SMEM = pl.BlockSpec(memory_space=pltpu.SMEM)


def blk_index(z, y, core):
    return (z % RING) * 4 + (y % 2) * 2 + core % 2


def rep_index(x, y):
    return (y % 2) * RING + x % RING


def blk_links():
    spots = [(z, y, c) for z in range(RING) for y in range(2) for c in range(2)]

    def link(dz, dy, dc):
        pairs = [(blk_index(z, y, c), blk_index(z + dz, y + dy, c + dc)) for z, y, c in spots]
        return lambda value: lax.ppermute(value, "blk", pairs)

    return link(1, 0, 0), link(-1, 0, 0), link(0, 1, 0), link(0, 0, 1)


def rep_links():
    spots = [(x, y) for x in range(RING) for y in range(2)]

    def link(dx, dy):
        pairs = [(rep_index(x, y), rep_index(x + dx, y + dy)) for x, y in spots]
        return lambda value: lax.ppermute(value, "rep", pairs)

    return link(1, 0), link(-1, 0), link(0, 1)


def nothing(*refs):
    pass


def together(*arrays):
    count = len(arrays)
    return pl.pallas_call(
        nothing,
        in_specs=[ANY] * count,
        out_specs=[ANY] * count,
        out_shape=[jax.ShapeDtypeStruct(a.shape, a.dtype) for a in arrays],
        input_output_aliases={i: i for i in range(count)},
        name="together",
    )(*arrays)


def gather_tree(own, up, down, pair, beside_it=lambda: ()):
    half = own.shape[0] // 2
    below, above, beside = together(up(own), down(own), pair(own))
    below_beside, above_beside, far, *others = together(
        pair(below), down(beside), up(below), *beside_it()
    )
    far_beside = [(0, down(above_beside[:half])), (half, up(below_beside[half:]))]
    whole = {
        (0, 0): own,
        (-1, 0): below,
        (1, 0): above,
        (0, 1): beside,
        (-1, 1): below_beside,
        (1, 1): above_beside,
        (2, 0): far,
    }
    return [far_beside if place == (2, 1) else [(0, whole[place])] for place in PLACES], others


def scatter_first(corner, blocks, up, down):
    low, high = (part.astype(BF16) for part in corner)
    half = low.shape[0]
    none = ((0, 0), (0, 0))
    low, high = together(up(low), down(high))
    above_beside = blocks[1, 1].astype(F32) + jnp.pad(low.astype(F32), ((0, half), *none))
    below_beside = blocks[-1, 1].astype(F32) + jnp.pad(high.astype(F32), ((half, 0), *none))
    return above_beside.astype(BF16), below_beside.astype(BF16), blocks[2, 0].astype(BF16)


def scatter_second(leaving, blocks, up, down, pair, beside_it=()):
    above_beside, below_beside, far = leaving
    below_beside, far, above_beside, *others = together(
        pair(below_beside), down(far), up(above_beside), *beside_it
    )
    below = blocks[-1, 0].astype(F32) + below_beside.astype(F32) + far.astype(F32)
    beside = blocks[0, 1].astype(F32) + above_beside.astype(F32)
    return (below.astype(BF16), beside.astype(BF16), blocks[1, 0].astype(BF16)), others


def scatter_third(leaving, own, up, down, pair):
    below, beside, above = leaving
    above, below, beside = together(up(above), down(below), pair(beside))
    return own.astype(F32) + above.astype(F32) + below.astype(F32) + beside.astype(F32)


def run_list(first, last, tile_list, panel_list, key_list, multiply, acc_ref):
    def add_group(g, carry):
        products = [
            multiply(tile_list[g * GROUP + j], panel_list[g * GROUP + j]) for j in range(GROUP)
        ]
        for j in range(GROUP):
            acc_ref[key_list[g * GROUP + j]] += products[j]
        return carry

    lax.fori_loop(first, last, add_group, 0)


def zero_all(acc_ref):
    def zero(i, carry):
        acc_ref[i] = jnp.zeros(acc_ref.shape[1:], F32)
        return carry

    lax.fori_loop(0, acc_ref.shape[0], zero, 0)


def fill_tail(count, spare, tile_list, panel_list, key_list):
    for j in range(GROUP):
        tile_list[count + j] = 0
        panel_list[count + j] = 0
        key_list[count + j] = spare


def load_sources(layout, order_ref, tiles_ref, shard_refs, tiles_v, shards_v, tile_sem, part_sem, slots, col_tiles):
    copies, part = [], 0
    for i, firsts in enumerate(layout):
        own = [
            pltpu.make_async_copy(
                tiles_ref.at[order_ref[i]], tiles_v.at[pl.ds(i * slots, slots)], tile_sem.at[i]
            )
        ]
        for first in firsts:
            size = shard_refs[part].shape[0]
            own.append(
                pltpu.make_async_copy(
                    shard_refs[part],
                    shards_v.at[pl.ds(i * col_tiles + first, size)],
                    part_sem.at[part],
                )
            )
            part += 1
        for copy in own:
            copy.start()
        copies.append(own)
    return copies


def forward_products(copies, order_ref, rows_ref, cols_ref, counts_ref, tiles_v, shards_v, acc_ref, tile_list, panel_list, key_list):
    sources = len(copies)
    slots = rows_ref.shape[1]
    col_tiles = shards_v.shape[0] // sources
    spare = acc_ref.shape[0] - 1
    count, ends = jnp.int32(0), []
    for i in range(sources):
        source = order_ref[i]

        def enlist(k, count, i=i, source=source):
            tile_list[count] = i * slots + k
            panel_list[count] = i * col_tiles + cols_ref[source, k]
            key_list[count] = rows_ref[source, k]
            return count + 1

        count = lax.fori_loop(0, counts_ref[source], enlist, count)
        ends.append(count)
    fill_tail(count, spare, tile_list, panel_list, key_list)

    def multiply(tile, panel):
        return jnp.dot(tiles_v[tile], shards_v[panel], preferred_element_type=F32)

    lists = (tile_list, panel_list, key_list, multiply, acc_ref)
    half = sources // 2
    for own in copies[:half]:
        for copy in own:
            copy.wait()
    middle = ends[half - 1] // GROUP
    run_list(0, middle, *lists)
    for own in copies[half:]:
        for copy in own:
            copy.wait()
    run_list(middle, (count + GROUP - 1) // GROUP, *lists)


def forward_kernel(layout, order_ref, dest_ref, rows_ref, cols_ref, counts_ref, tiles_ref, *refs):
    parts = sum(len(firsts) for firsts in layout)
    shard_refs, refs = refs[:parts], refs[parts:]
    out_refs, offset_ref, refs = refs[: len(PLACES) + 1], refs[len(PLACES) + 1], refs[len(PLACES) + 2 :]
    acc_ref, tiles_v, shards_v, *lists, tile_sem, part_sem = refs
    slots, col_tiles = rows_ref.shape[1], shards_v.shape[0] // len(layout)
    row_tiles = acc_ref.shape[0] - 1
    copies = load_sources(
        layout, order_ref, tiles_ref, shard_refs, tiles_v, shards_v, tile_sem, part_sem, slots, col_tiles
    )
    zero_all(acc_ref)
    forward_products(
        copies, order_ref, rows_ref, cols_ref, counts_ref, tiles_v, shards_v, acc_ref, *lists
    )

    def total(i, carry):
        return carry + jnp.sum(acc_ref[i].reshape(-1, 8, acc_ref.shape[2]), axis=0)

    sums = lax.fori_loop(0, row_tiles, total, jnp.zeros((8, acc_ref.shape[2]), F32))
    offset = jnp.sum(sums, axis=0, keepdims=True) / (row_tiles * acc_ref.shape[1])
    offset_ref[...] = offset
    half = col_tiles // 2
    spans = [(out_refs[0], 0, 0, half), (out_refs[1], 0, half, half)]
    spans += [(out_refs[d + 1], d, 0, col_tiles) for d in range(1, len(PLACES))]
    for out_ref, d, first, size in spans:
        base = dest_ref[d] * col_tiles + first

        def put(i, carry, out_ref=out_ref, base=base):
            out_ref[i] = (acc_ref[base + i] - offset).astype(BF16)
            return carry

        lax.fori_loop(0, size, put, 0)


def list_shapes(cap):
    return [pltpu.SMEM((cap,), jnp.int32)] * 3


def forward_tiles(order, dests, scalars, tiles, shards):
    arrays = [array for parts in shards for _, array in parts]
    layout = tuple(tuple(first for first, _ in parts) for parts in shards)
    sources, slots, tile, _ = tiles.shape
    width = arrays[0].shape[2]
    col_tiles = sum(array.shape[0] for _, array in shards[0])
    row_tiles = col_tiles * len(PLACES)
    sizes = [col_tiles // 2] * 2 + [col_tiles] * (len(PLACES) - 1)
    out_shape = [jax.ShapeDtypeStruct((size, tile, width), BF16) for size in sizes]
    out_shape.append(jax.ShapeDtypeStruct((1, width), F32))
    return pl.pallas_call(
        functools.partial(forward_kernel, layout),
        in_specs=[SMEM] * 5 + [ANY] * (1 + len(arrays)),
        out_specs=[VMEM] * len(out_shape),
        out_shape=out_shape,
        scratch_shapes=[
            pltpu.VMEM((row_tiles + 1, tile, width), F32),
            pltpu.VMEM((sources * slots, tile, tile), BF16),
            pltpu.VMEM((sources * col_tiles, tile, width), BF16),
            *list_shapes(sources * slots + GROUP),
            pltpu.SemaphoreType.DMA((sources,)),
            pltpu.SemaphoreType.DMA((len(arrays),)),
        ],
        compiler_params=pltpu.CompilerParams(vmem_limit_bytes=44 * 2**20),
        cost_estimate=pl.CostEstimate(flops=6 * 10**9, bytes_accessed=30 * 2**20, transcendentals=0),
        name="forward_tiles",
    )(order, dests, *scalars, tiles, *arrays)


def backward_kernel(layout, sizes, waits, order_ref, dest_ref, rows_ref, cols_ref, counts_ref, tiles_ref, *refs):
    parts = sum(len(firsts) for firsts in layout)
    grad_refs, refs = refs[:parts], refs[parts + waits :]
    out_refs, refs = refs[: len(sizes)], refs[len(sizes) :]
    tiles_v, grads_v, acc_ref, tile_list, panel_list, key_list, tile_sem, part_sem = refs
    slots = rows_ref.shape[1]
    sources = tiles_v.shape[0] // slots
    col_tiles = (acc_ref.shape[0] - 1) // sources

    copies, part = [], 0
    for i, firsts in enumerate(layout):
        base = dest_ref[i] * col_tiles
        for first in firsts:
            size = grad_refs[part].shape[0]
            copies.append(
                pltpu.make_async_copy(
                    grad_refs[part], grads_v.at[pl.ds(base + first, size)], part_sem.at[part]
                )
            )
            part += 1
    tile_copies = [
        pltpu.make_async_copy(
            tiles_ref.at[order_ref[i]], tiles_v.at[pl.ds(i * slots, slots)], tile_sem.at[i]
        )
        for i in range(sources)
    ]
    for copy in copies + tile_copies:
        copy.start()

    zero_all(acc_ref)
    count, ends = jnp.int32(0), []
    for i in range(sources):
        source = order_ref[i]

        def enlist(k, count, i=i, source=source):
            tile_list[count] = i * slots + k
            panel_list[count] = rows_ref[source, k]
            key_list[count] = i * col_tiles + cols_ref[source, k]
            return count + 1

        count = lax.fori_loop(0, counts_ref[source], enlist, count)
        ends.append(count)
    fill_tail(count, sources * col_tiles, tile_list, panel_list, key_list)

    def multiply(tile, panel):
        return lax.dot_general(
            tiles_v[tile], grads_v[panel], (((0,), (0,)), ((), ())), preferred_element_type=F32
        )

    lists = (tile_list, panel_list, key_list, multiply, acc_ref)
    for copy in copies + tile_copies[: sources // 2]:
        copy.wait()
    middle = ends[sources // 2 - 1] // GROUP
    run_list(0, middle, *lists)
    for copy in tile_copies[sources // 2 :]:
        copy.wait()
    run_list(middle, (count + GROUP - 1) // GROUP, *lists)

    base = 0
    for out_ref, size in zip(out_refs, sizes):

        def put(t, carry, out_ref=out_ref, base=base):
            out_ref[t] = acc_ref[base + t].astype(BF16)
            return carry

        lax.fori_loop(0, size, put, 0)
        base += size


def backward_tiles(sizes, order, dests, scalars, tiles, grads, after=()):
    arrays = [array for parts in grads for _, array in parts]
    layout = tuple(tuple(first for first, _ in parts) for parts in grads)
    slots, tile = tiles.shape[1:3]
    width = arrays[0].shape[2]
    row_tiles = sum(array.shape[0] for array in arrays)
    sources = order.shape[0]
    return pl.pallas_call(
        functools.partial(backward_kernel, layout, sizes, len(after)),
        in_specs=[SMEM] * 5 + [ANY] * (1 + len(arrays) + len(after)),
        out_specs=[VMEM] * len(sizes),
        out_shape=[jax.ShapeDtypeStruct((size, tile, width), BF16) for size in sizes],
        scratch_shapes=[
            pltpu.VMEM((sources * slots, tile, tile), BF16),
            pltpu.VMEM((row_tiles, tile, width), BF16),
            pltpu.VMEM((sum(sizes) + 1, tile, width), F32),
            *list_shapes(sources * slots + GROUP),
            pltpu.SemaphoreType.DMA((sources,)),
            pltpu.SemaphoreType.DMA((len(arrays),)),
        ],
        compiler_params=pltpu.CompilerParams(vmem_limit_bytes=52 * 2**20),
        cost_estimate=pl.CostEstimate(flops=8 * 10**9, bytes_accessed=20 * 2**20, transcendentals=0),
        name="backward_tiles",
    )(order, dests, *scalars, tiles, *arrays, *after)


def weight_kernel(aggregate_ref, grad_ref, offset_ref, *refs):
    grads = grad_ref[...]
    sums = jnp.sum(grads.astype(F32), axis=0, keepdims=True)
    refs[-1][...] = (
        lax.dot_general(
            aggregate_ref[...], grads, (((0,), (0,)), ((), ())), preferred_element_type=F32
        )
        + offset_ref[...] * sums
    )


def weight_terms(aggregate, grads, offset, after):
    width = grads.shape[1]
    return pl.pallas_call(
        weight_kernel,
        in_specs=[VMEM] * 3 + [ANY] * len(after),
        out_specs=VMEM,
        out_shape=jax.ShapeDtypeStruct((width, width), F32),
        name="weight_terms",
    )(aggregate, grads, jnp.broadcast_to(offset[:, None], (width, width)), *after)


def copies_of_all(value, axis):
    count = lax.axis_size(axis)
    return lax.all_to_all(jnp.broadcast_to(value[None], (count, *value.shape)), axis, 0, 0)


def on_device(
    features,
    weight,
    norm_gain,
    norm_shift,
    tile_values,
    tile_rows,
    tile_cols,
    tile_counts,
    cotangent,
):
    tiles, rows, cols, counts = tile_values[0], tile_rows[0], tile_cols[0], tile_counts[0]
    local_rows, width = features.shape
    tile = tiles.shape[-1]
    col_tiles = local_rows // tile
    blk_count = lax.axis_size("blk")
    rep_count = lax.axis_size("rep")
    node_count = local_rows * blk_count * rep_count
    blk, rep = lax.axis_index("blk"), lax.axis_index("rep")
    z, y_low, core = blk // 4, (blk // 2) % 2, blk % 2
    y_high, x = rep // RING, rep % RING
    own_core = jnp.stack([blk_index(z + a + RING, y_low + b, core) for a, b in PLACES])
    other_core = own_core + (1 - 2 * core)
    dests = jnp.stack([rep_index(x + a + RING, y_high + b) for a, b in PLACES])
    *blk_tree, across = blk_links()
    rep_tree = rep_links()

    mine, _ = gather_tree(features.reshape(col_tiles, tile, width), *blk_tree)
    theirs = [[(first, across(array)) for first, array in parts] for parts in mine]
    backwards = slice(None, None, -1)
    scalars = (rows, cols, counts)
    order = jnp.stack([own_core[backwards], other_core[backwards]], axis=1).reshape(-1)
    shards = [parts for both in zip(mine[backwards], theirs[backwards]) for parts in both]
    up, down, pair = rep_tree
    low, high, *rest, offset = forward_tiles(order, dests, scalars, tiles, shards)
    blocks = dict(zip(PLACES[1:], rest))
    leaving = scatter_first((low, high), blocks, up, down)
    leaving, _ = scatter_second(leaving, blocks, *rep_tree)
    shifted = scatter_third(leaving, blocks[0, 0], *rep_tree).reshape(local_rows, width)
    aggregate = shifted.astype(BF16)
    projected = jnp.dot(aggregate, weight, preferred_element_type=F32)
    own_mean = jnp.sum(projected, axis=0) / local_rows
    own_square = jnp.sum((projected - own_mean) ** 2, axis=0)
    moved = jnp.dot(offset, weight.astype(F32), precision=lax.Precision.HIGHEST)
    everyone = copies_of_all(
        jnp.stack([own_mean, own_square, moved[0], offset[0]]), ("blk", "rep")
    ).reshape(blk_count, rep_count, 4, width)
    moves = jnp.sum(everyone[:, :, 2], axis=1)
    means = everyone[:, :, 0] + moves[:, None]
    feat_mean = jnp.sum(means, axis=(0, 1)) / (blk_count * rep_count)
    square_sum = jnp.sum(everyone[:, :, 1], axis=(0, 1)) + local_rows * jnp.sum(
        (means - feat_mean) ** 2, axis=(0, 1)
    )
    group = lax.dynamic_index_in_dim(everyone, blk, 0, keepdims=False)
    group_moved, group_offset = jnp.sum(group[:, 2], axis=0), jnp.sum(group[:, 3], axis=0)
    inv_std = lax.rsqrt(square_sum / node_count + norm_eps)
    normed = (projected + (group_moved - feat_mean)) * inv_std
    affine = norm_gain * normed + norm_shift
    gate_value = jax.nn.sigmoid(affine)
    output = (affine * gate_value).astype(BF16)
    grad_affine = cotangent.astype(F32) * gate_value * (1.0 + affine * (1.0 - gate_value))
    grad_beta, grad_gamma = jnp.sum(
        copies_of_all(
            jnp.stack([jnp.sum(grad_affine, axis=0), jnp.sum(grad_affine * normed, axis=0)]),
            ("blk", "rep"),
        ),
        axis=0,
    )
    grad_summed = (
        norm_gain
        * inv_std
        * (grad_affine - grad_beta / node_count - normed * grad_gamma / node_count)
    ).astype(BF16)

    sent = lax.dot_general(
        grad_summed, weight, (((1,), (1,)), ((), ())), preferred_element_type=F32
    ).astype(BF16)
    def weight_pieces():
        term = weight_terms(aggregate, grad_summed, group_offset, [])
        return [lax.all_to_all(term.reshape(blk_count, -1, width), "blk", 0, 0)]

    grads, [pieces] = gather_tree(
        sent.reshape(col_tiles, tile, width), *rep_tree, weight_pieces
    )
    piece = jnp.sum(pieces, axis=0)
    terms = copies_of_all(piece, "rep")

    half = col_tiles // 2
    sizes = (half, half, *(col_tiles,) * (len(PLACES) - 1))
    arrays = backward_tiles(
        sizes * 2,
        jnp.concatenate([other_core, own_core]),
        dests,
        scalars,
        tiles,
        grads,
    )
    given, kept = arrays[: len(sizes)], arrays[len(sizes) :]
    low, high, *rest = [b.astype(F32) + across(a).astype(F32) for a, b in zip(given, kept)]
    products = dict(zip(PLACES[1:], rest))
    up, down, pair = blk_tree
    leaving = scatter_first((low, high), products, up, down)
    leaving, [terms] = scatter_second(leaving, products, *blk_tree, [terms])
    grad_x = scatter_third(leaving, products[0, 0], *blk_tree).astype(BF16)
    grad_w = copies_of_all(jnp.sum(terms, axis=0), "blk").reshape(weight.shape)
    return (output, grad_x.reshape(local_rows, width), grad_w, grad_gamma, grad_beta)


def solution(mesh):
    return jax.shard_map(
        on_device,
        mesh=mesh,
        in_specs=(
            P(("blk", "rep"), None),
            P(),
            P(),
            P(),
            P("blk", "rep", None, None, None),
            P("blk", "rep", None),
            P("blk", "rep", None),
            P("blk", "rep"),
            P(("blk", "rep"), None),
        ),
        out_specs=(P(("blk", "rep"), None), P(("blk", "rep"), None), P(), P(), P()),
        check_vma=False,
    )
```

```python
import functools

import jax
import jax.numpy as jnp
from jax import lax
from jax.experimental import pallas as pl
from jax.experimental.pallas import tpu as pltpu
from jax.sharding import PartitionSpec as P

norm_eps = 1e-05
GROUP = 32
BF16, F32 = jnp.bfloat16, jnp.float32
VMEM_LIMIT = 60 * 2**20
ENLIST = 4
RING = 4
PLACES = ((2, 1), (1, 1), (-1, 1), (2, 0), (0, 1), (1, 0), (-1, 0), (0, 0))
ANY = pl.BlockSpec(memory_space=pl.ANY)
VMEM = pl.BlockSpec(memory_space=pltpu.VMEM)
SMEM = pl.BlockSpec(memory_space=pltpu.SMEM)


def blk_index(z, y, core):
    return (z % RING) * 4 + (y % 2) * 2 + core % 2


def rep_index(x, y):
    return (y % 2) * RING + x % RING


def blk_links():
    spots = [(z, y, c) for z in range(RING) for y in range(2) for c in range(2)]

    def link(dz, dy, dc):
        pairs = [(blk_index(z, y, c), blk_index(z + dz, y + dy, c + dc)) for z, y, c in spots]
        return lambda value: lax.ppermute(value, "blk", pairs)

    return link(1, 0, 0), link(-1, 0, 0), link(0, 1, 0), link(0, 0, 1)


def rep_links():
    spots = [(x, y) for x in range(RING) for y in range(2)]

    def link(dx, dy):
        pairs = [(rep_index(x, y), rep_index(x + dx, y + dy)) for x, y in spots]
        return lambda value: lax.ppermute(value, "rep", pairs)

    return link(1, 0), link(-1, 0), link(0, 1)


def nothing(*refs):
    pass


def together(*arrays):
    count = len(arrays)
    return pl.pallas_call(
        nothing,
        in_specs=[ANY] * count,
        out_specs=[ANY] * count,
        out_shape=[jax.ShapeDtypeStruct(a.shape, a.dtype) for a in arrays],
        input_output_aliases={i: i for i in range(count)},
        name="together",
    )(*arrays)


def gather_tree(own, up, down, pair):
    half = own.shape[0] // 2
    below, above, beside = up(own), down(own), pair(own)
    below_beside, above_beside, far = pair(below), down(beside), up(below)
    far_beside = [(0, down(above_beside[:half])), (half, up(below_beside[half:]))]
    whole = {
        (0, 0): own,
        (-1, 0): below,
        (1, 0): above,
        (0, 1): beside,
        (-1, 1): below_beside,
        (1, 1): above_beside,
        (2, 0): far,
    }
    return [far_beside if place == (2, 1) else [(0, whole[place])] for place in PLACES]


def scatter_first(corner, blocks, up, down):
    low, high = (part.astype(BF16) for part in corner)
    half = low.shape[0]
    none = ((0, 0), (0, 0))
    low, high = together(up(low), down(high))
    above_beside = blocks[1, 1].astype(F32) + jnp.pad(low.astype(F32), ((0, half), *none))
    below_beside = blocks[-1, 1].astype(F32) + jnp.pad(high.astype(F32), ((half, 0), *none))
    return above_beside.astype(BF16), below_beside.astype(BF16), blocks[2, 0].astype(BF16)


def scatter_second(leaving, blocks, up, down, pair):
    above_beside, below_beside, far = leaving
    below = blocks[-1, 0].astype(F32) + pair(below_beside).astype(F32) + down(far).astype(F32)
    beside = blocks[0, 1].astype(F32) + up(above_beside).astype(F32)
    return below.astype(BF16), beside.astype(BF16), blocks[1, 0].astype(BF16)


def scatter_third(leaving, own, up, down, pair):
    below, beside, above = leaving
    return (
        own.astype(F32)
        + up(above).astype(F32)
        + down(below).astype(F32)
        + pair(beside).astype(F32)
    )


def run_list(first, last, tile_list, panel_list, key_list, multiply, acc_ref):
    def add_group(g, carry):
        products = [
            multiply(tile_list[g * GROUP + j], panel_list[g * GROUP + j]) for j in range(GROUP)
        ]
        for j in range(GROUP):
            acc_ref[key_list[g * GROUP + j]] += products[j]
        return carry

    lax.fori_loop(first, last, add_group, 0)


def zero_all(acc_ref):
    def zero(i, carry):
        acc_ref[i] = jnp.zeros(acc_ref.shape[1:], F32)
        return carry

    lax.fori_loop(0, acc_ref.shape[0], zero, 0)


def fill_tail(count, spare, tile_list, panel_list, key_list):
    for j in range(GROUP):
        tile_list[count + j] = 0
        panel_list[count + j] = 0
        key_list[count + j] = spare


def load_sources(layout, order_ref, tiles_ref, shard_refs, tiles_v, shards_v, tile_sem, part_sem, slots, col_tiles):
    copies, part = [], 0
    for i, firsts in enumerate(layout):
        own = [
            pltpu.make_async_copy(
                tiles_ref.at[order_ref[i]], tiles_v.at[pl.ds(i * slots, slots)], tile_sem.at[i]
            )
        ]
        for first in firsts:
            size = shard_refs[part].shape[0]
            own.append(
                pltpu.make_async_copy(
                    shard_refs[part],
                    shards_v.at[pl.ds(i * col_tiles + first, size)],
                    part_sem.at[part],
                )
            )
            part += 1
        for copy in own:
            copy.start()
        copies.append(own)
    return copies


def forward_products(copies, order_ref, rows_ref, cols_ref, counts_ref, tiles_v, shards_v, acc_ref, tile_list, panel_list, key_list):
    sources = len(copies)
    slots = rows_ref.shape[1]
    col_tiles = shards_v.shape[0] // sources
    spare = acc_ref.shape[0] - 1
    count, ends = jnp.int32(0), []
    for i in range(sources):
        source = order_ref[i]

        def enlist(g, count, i=i, source=source):
            for j in range(ENLIST):
                k = g * ENLIST + j
                tile_list[count + j] = i * slots + k
                panel_list[count + j] = i * col_tiles + cols_ref[source, k]
                key_list[count + j] = rows_ref[source, k]
            return count + jnp.minimum(ENLIST, counts_ref[source] - g * ENLIST)

        count = lax.fori_loop(0, (counts_ref[source] + ENLIST - 1) // ENLIST, enlist, count)
        ends.append(count)
    fill_tail(count, spare, tile_list, panel_list, key_list)

    def multiply(tile, panel):
        return jnp.dot(tiles_v[tile], shards_v[panel], preferred_element_type=F32)

    lists = (tile_list, panel_list, key_list, multiply, acc_ref)
    half = sources // 2
    for own in copies[:half]:
        for copy in own:
            copy.wait()
    middle = ends[half - 1] // GROUP
    run_list(0, middle, *lists)
    for own in copies[half:]:
        for copy in own:
            copy.wait()
    run_list(middle, (count + GROUP - 1) // GROUP, *lists)


def forward_kernel(layout, order_ref, dest_ref, rows_ref, cols_ref, counts_ref, tiles_ref, *refs):
    parts = sum(len(firsts) for firsts in layout)
    shard_refs, refs = refs[:parts], refs[parts:]
    out_refs, offset_ref, refs = refs[: len(PLACES) + 1], refs[len(PLACES) + 1], refs[len(PLACES) + 2 :]
    acc_ref, tiles_v, shards_v, *lists, tile_sem, part_sem = refs
    slots, col_tiles = rows_ref.shape[1], shards_v.shape[0] // len(layout)
    row_tiles = acc_ref.shape[0] - 1
    copies = load_sources(
        layout, order_ref, tiles_ref, shard_refs, tiles_v, shards_v, tile_sem, part_sem, slots, col_tiles
    )
    zero_all(acc_ref)
    forward_products(
        copies, order_ref, rows_ref, cols_ref, counts_ref, tiles_v, shards_v, acc_ref, *lists
    )

    def total(i, carry):
        return carry + jnp.sum(acc_ref[i].reshape(-1, 8, acc_ref.shape[2]), axis=0)

    sums = lax.fori_loop(0, row_tiles, total, jnp.zeros((8, acc_ref.shape[2]), F32))
    offset = jnp.sum(sums, axis=0, keepdims=True) / (row_tiles * acc_ref.shape[1])
    offset_ref[...] = offset
    half = col_tiles // 2
    spans = [(out_refs[0], 0, 0, half), (out_refs[1], 0, half, half)]
    spans += [(out_refs[d + 1], d, 0, col_tiles) for d in range(1, len(PLACES))]
    for out_ref, d, first, size in spans:
        base = dest_ref[d] * col_tiles + first

        def put(i, carry, out_ref=out_ref, base=base):
            out_ref[i] = (acc_ref[base + i] - offset).astype(BF16)
            return carry

        lax.fori_loop(0, size, put, 0)


def list_shapes(cap):
    return [pltpu.SMEM((cap,), jnp.int32)] * 3


def forward_tiles(order, dests, scalars, tiles, shards):
    arrays = [array for parts in shards for _, array in parts]
    layout = tuple(tuple(first for first, _ in parts) for parts in shards)
    sources, slots, tile, _ = tiles.shape
    width = arrays[0].shape[2]
    col_tiles = sum(array.shape[0] for _, array in shards[0])
    row_tiles = col_tiles * len(PLACES)
    sizes = [col_tiles // 2] * 2 + [col_tiles] * (len(PLACES) - 1)
    out_shape = [jax.ShapeDtypeStruct((size, tile, width), BF16) for size in sizes]
    out_shape.append(jax.ShapeDtypeStruct((1, width), F32))
    return pl.pallas_call(
        functools.partial(forward_kernel, layout),
        in_specs=[SMEM] * 5 + [ANY] * (1 + len(arrays)),
        out_specs=[VMEM] * len(out_shape),
        out_shape=out_shape,
        scratch_shapes=[
            pltpu.VMEM((row_tiles + 1, tile, width), F32),
            pltpu.VMEM((sources * slots, tile, tile), BF16),
            pltpu.VMEM((sources * col_tiles, tile, width), BF16),
            *list_shapes(sources * slots + GROUP),
            pltpu.SemaphoreType.DMA((sources,)),
            pltpu.SemaphoreType.DMA((len(arrays),)),
        ],
        compiler_params=pltpu.CompilerParams(vmem_limit_bytes=VMEM_LIMIT),
        cost_estimate=pl.CostEstimate(flops=6 * 10**9, bytes_accessed=30 * 2**20, transcendentals=0),
        name="forward_tiles",
    )(order, dests, *scalars, tiles, *arrays)


def backward_kernel(layout, sizes, waits, order_ref, dest_ref, rows_ref, cols_ref, counts_ref, tiles_ref, *refs):
    parts = sum(len(firsts) for firsts in layout)
    grad_refs, refs = refs[:parts], refs[parts + waits :]
    out_refs, refs = refs[: len(sizes)], refs[len(sizes) :]
    tiles_v, grads_v, acc_ref, tile_list, panel_list, key_list, tile_sem, part_sem = refs
    slots = rows_ref.shape[1]
    sources = tiles_v.shape[0] // slots
    col_tiles = (acc_ref.shape[0] - 1) // sources

    copies, part = [], 0
    for i, firsts in enumerate(layout):
        base = dest_ref[i] * col_tiles
        for first in firsts:
            size = grad_refs[part].shape[0]
            copies.append(
                pltpu.make_async_copy(
                    grad_refs[part], grads_v.at[pl.ds(base + first, size)], part_sem.at[part]
                )
            )
            part += 1
    tile_copies = [
        pltpu.make_async_copy(
            tiles_ref.at[order_ref[i]], tiles_v.at[pl.ds(i * slots, slots)], tile_sem.at[i]
        )
        for i in range(sources)
    ]
    for copy in copies + tile_copies:
        copy.start()

    zero_all(acc_ref)
    count, ends = jnp.int32(0), []
    for i in range(sources):
        source = order_ref[i]

        def enlist(g, count, i=i, source=source):
            for j in range(ENLIST):
                k = g * ENLIST + j
                tile_list[count + j] = i * slots + k
                panel_list[count + j] = rows_ref[source, k]
                key_list[count + j] = i * col_tiles + cols_ref[source, k]
            return count + jnp.minimum(ENLIST, counts_ref[source] - g * ENLIST)

        count = lax.fori_loop(0, (counts_ref[source] + ENLIST - 1) // ENLIST, enlist, count)
        ends.append(count)
    fill_tail(count, sources * col_tiles, tile_list, panel_list, key_list)

    def multiply(tile, panel):
        return lax.dot_general(
            tiles_v[tile], grads_v[panel], (((0,), (0,)), ((), ())), preferred_element_type=F32
        )

    lists = (tile_list, panel_list, key_list, multiply, acc_ref)
    for copy in copies + tile_copies[: sources // 2]:
        copy.wait()
    middle = ends[sources // 2 - 1] // GROUP
    run_list(0, middle, *lists)
    for copy in tile_copies[sources // 2 :]:
        copy.wait()
    run_list(middle, (count + GROUP - 1) // GROUP, *lists)

    base = 0
    for out_ref, size in zip(out_refs, sizes):

        def put(t, carry, out_ref=out_ref, base=base):
            out_ref[t] = acc_ref[base + t].astype(BF16)
            return carry

        lax.fori_loop(0, size, put, 0)
        base += size


def backward_tiles(sizes, order, dests, scalars, tiles, grads, after=()):
    arrays = [array for parts in grads for _, array in parts]
    layout = tuple(tuple(first for first, _ in parts) for parts in grads)
    slots, tile = tiles.shape[1:3]
    width = arrays[0].shape[2]
    row_tiles = sum(array.shape[0] for array in arrays)
    sources = order.shape[0]
    return pl.pallas_call(
        functools.partial(backward_kernel, layout, sizes, len(after)),
        in_specs=[SMEM] * 5 + [ANY] * (1 + len(arrays) + len(after)),
        out_specs=[VMEM] * len(sizes),
        out_shape=[jax.ShapeDtypeStruct((size, tile, width), BF16) for size in sizes],
        scratch_shapes=[
            pltpu.VMEM((sources * slots, tile, tile), BF16),
            pltpu.VMEM((row_tiles, tile, width), BF16),
            pltpu.VMEM((sum(sizes) + 1, tile, width), F32),
            *list_shapes(sources * slots + GROUP),
            pltpu.SemaphoreType.DMA((sources,)),
            pltpu.SemaphoreType.DMA((len(arrays),)),
        ],
        compiler_params=pltpu.CompilerParams(vmem_limit_bytes=VMEM_LIMIT),
        cost_estimate=pl.CostEstimate(flops=8 * 10**9, bytes_accessed=20 * 2**20, transcendentals=0),
        name="backward_tiles",
    )(order, dests, *scalars, tiles, *arrays, *after)


def sum_first_kernel(value_ref, *refs):
    refs[-1][...] = jnp.sum(value_ref[...], axis=0)


def sum_first(value, after):
    return pl.pallas_call(
        sum_first_kernel,
        in_specs=[VMEM] + [ANY] * len(after),
        out_specs=VMEM,
        out_shape=jax.ShapeDtypeStruct(value.shape[1:], value.dtype),
        name="sum_first",
    )(value, *after)


def weight_kernel(aggregate_ref, grad_ref, offset_ref, *refs):
    grads = grad_ref[...]
    sums = jnp.sum(grads.astype(F32), axis=0, keepdims=True)
    refs[-1][...] = (
        lax.dot_general(
            aggregate_ref[...], grads, (((0,), (0,)), ((), ())), preferred_element_type=F32
        )
        + offset_ref[...] * sums
    )


def weight_terms(aggregate, grads, offset, after):
    width = grads.shape[1]
    return pl.pallas_call(
        weight_kernel,
        in_specs=[VMEM] * 3 + [ANY] * len(after),
        out_specs=VMEM,
        out_shape=jax.ShapeDtypeStruct((width, width), F32),
        name="weight_terms",
    )(aggregate, grads, jnp.broadcast_to(offset[:, None], (width, width)), *after)


def copies_of_all(value, axis):
    count = lax.axis_size(axis)
    return lax.all_to_all(jnp.broadcast_to(value[None], (count, *value.shape)), axis, 0, 0)


def on_device(
    features,
    weight,
    norm_gain,
    norm_shift,
    tile_values,
    tile_rows,
    tile_cols,
    tile_counts,
    cotangent,
):
    tiles, rows, cols, counts = tile_values[0], tile_rows[0], tile_cols[0], tile_counts[0]
    local_rows, width = features.shape
    tile = tiles.shape[-1]
    col_tiles = local_rows // tile
    blk_count = lax.axis_size("blk")
    rep_count = lax.axis_size("rep")
    node_count = local_rows * blk_count * rep_count
    blk, rep = lax.axis_index("blk"), lax.axis_index("rep")
    z, y_low, core = blk // 4, (blk // 2) % 2, blk % 2
    y_high, x = rep // RING, rep % RING
    own_core = jnp.stack([blk_index(z + a + RING, y_low + b, core) for a, b in PLACES])
    other_core = own_core + (1 - 2 * core)
    dests = jnp.stack([rep_index(x + a + RING, y_high + b) for a, b in PLACES])
    *blk_tree, across = blk_links()
    rep_tree = rep_links()

    mine = gather_tree(features.reshape(col_tiles, tile, width), *blk_tree)
    theirs = [[(first, across(array)) for first, array in parts] for parts in mine]
    backwards = slice(None, None, -1)
    scalars = (rows, cols, counts)
    order = jnp.stack([own_core[backwards], other_core[backwards]], axis=1).reshape(-1)
    shards = [parts for both in zip(mine[backwards], theirs[backwards]) for parts in both]
    up, down, pair = rep_tree
    low, high, *rest, offset = forward_tiles(order, dests, scalars, tiles, shards)
    blocks = dict(zip(PLACES[1:], rest))
    leaving = scatter_first((low, high), blocks, up, down)
    leaving = scatter_second(leaving, blocks, *rep_tree)
    shifted = scatter_third(leaving, blocks[0, 0], *rep_tree).reshape(local_rows, width)
    aggregate = shifted.astype(BF16)
    projected = jnp.dot(aggregate, weight, preferred_element_type=F32)
    own_mean = jnp.sum(projected, axis=0) / local_rows
    own_square = jnp.sum((projected - own_mean) ** 2, axis=0)
    moved = jnp.dot(offset, weight.astype(F32), precision=lax.Precision.HIGHEST)
    everyone = copies_of_all(
        jnp.stack([own_mean, own_square, moved[0], offset[0]]), ("blk", "rep")
    ).reshape(blk_count, rep_count, 4, width)
    moves = jnp.sum(everyone[:, :, 2], axis=1)
    means = everyone[:, :, 0] + moves[:, None]
    feat_mean = jnp.sum(means, axis=(0, 1)) / (blk_count * rep_count)
    square_sum = jnp.sum(everyone[:, :, 1], axis=(0, 1)) + local_rows * jnp.sum(
        (means - feat_mean) ** 2, axis=(0, 1)
    )
    group = lax.dynamic_index_in_dim(everyone, blk, 0, keepdims=False)
    group_moved, group_offset = jnp.sum(group[:, 2], axis=0), jnp.sum(group[:, 3], axis=0)
    inv_std = lax.rsqrt(square_sum / node_count + norm_eps)
    normed = (projected + (group_moved - feat_mean)) * inv_std
    affine = norm_gain * normed + norm_shift
    gate_value = jax.nn.sigmoid(affine)
    output = (affine * gate_value).astype(BF16)
    grad_affine = cotangent.astype(F32) * gate_value * (1.0 + affine * (1.0 - gate_value))
    grad_beta, grad_gamma = jnp.sum(
        copies_of_all(
            jnp.stack([jnp.sum(grad_affine, axis=0), jnp.sum(grad_affine * normed, axis=0)]),
            ("blk", "rep"),
        ),
        axis=0,
    )
    grad_summed = (
        norm_gain
        * inv_std
        * (grad_affine - grad_beta / node_count - normed * grad_gamma / node_count)
    ).astype(BF16)

    sent = lax.dot_general(
        grad_summed, weight, (((1,), (1,)), ((), ())), preferred_element_type=F32
    ).astype(BF16)
    grads = gather_tree(sent.reshape(col_tiles, tile, width), *rep_tree)
    arrived = {place: parts[0][1] for place, parts in zip(PLACES, grads)}
    weight_term = weight_terms(aggregate, grad_summed, group_offset, [arrived[1, 0]])
    pieces = lax.all_to_all(weight_term.reshape(blk_count, -1, width), "blk", 0, 0)
    piece = sum_first(pieces, [arrived[-1, 1]])
    terms = copies_of_all(piece, "rep")

    half = col_tiles // 2
    sizes = (half, half, *(col_tiles,) * (len(PLACES) - 1))
    arrays = backward_tiles(
        sizes * 2,
        jnp.concatenate([other_core, own_core]),
        dests,
        scalars,
        tiles,
        grads,
        [terms],
    )
    given, kept = arrays[: len(sizes)], arrays[len(sizes) :]
    low, high, *rest = [b.astype(F32) + across(a).astype(F32) for a, b in zip(given, kept)]
    products = dict(zip(PLACES[1:], rest))
    up, down, pair = blk_tree
    leaving = scatter_first((low, high), products, up, down)
    leaving = scatter_second(leaving, products, *blk_tree)
    grad_w = copies_of_all(sum_first(terms, [leaving[0][:1, :16, :128]]), "blk")
    grad_x = scatter_third(leaving, products[0, 0], *blk_tree).astype(BF16)
    grad_w = grad_w.reshape(weight.shape)
    return (output, grad_x.reshape(local_rows, width), grad_w, grad_gamma, grad_beta)


def solution(mesh):
    return jax.shard_map(
        on_device,
        mesh=mesh,
        in_specs=(
            P(("blk", "rep"), None),
            P(),
            P(),
            P(),
            P("blk", "rep", None, None, None),
            P("blk", "rep", None),
            P("blk", "rep", None),
            P("blk", "rep"),
            P(("blk", "rep"), None),
        ),
        out_specs=(P(("blk", "rep"), None), P(("blk", "rep"), None), P(), P(), P()),
        check_vma=False,
    )
```

```python
import functools

import jax
import jax.numpy as jnp
from jax import lax
from jax.experimental import pallas as pl
from jax.experimental.pallas import tpu as pltpu
from jax.sharding import PartitionSpec as P

norm_eps = 1e-05
GROUP = 32
BF16, F32 = jnp.bfloat16, jnp.float32
VMEM_LIMIT = 60 * 2**20
RING = 4
PLACES = ((2, 1), (1, 1), (-1, 1), (2, 0), (0, 1), (1, 0), (-1, 0), (0, 0))
ANY = pl.BlockSpec(memory_space=pl.ANY)
VMEM = pl.BlockSpec(memory_space=pltpu.VMEM)
SMEM = pl.BlockSpec(memory_space=pltpu.SMEM)


def blk_index(z, y, core):
    return (z % RING) * 4 + (y % 2) * 2 + core % 2


def rep_index(x, y):
    return (y % 2) * RING + x % RING


def blk_links():
    spots = [(z, y, c) for z in range(RING) for y in range(2) for c in range(2)]

    def link(dz, dy, dc):
        pairs = [(blk_index(z, y, c), blk_index(z + dz, y + dy, c + dc)) for z, y, c in spots]
        return lambda value: lax.ppermute(value, "blk", pairs)

    return link(1, 0, 0), link(-1, 0, 0), link(0, 1, 0), link(0, 0, 1)


def rep_links():
    spots = [(x, y) for x in range(RING) for y in range(2)]

    def link(dx, dy):
        pairs = [(rep_index(x, y), rep_index(x + dx, y + dy)) for x, y in spots]
        return lambda value: lax.ppermute(value, "rep", pairs)

    return link(1, 0), link(-1, 0), link(0, 1)


def nothing(*refs):
    pass


def together(*arrays):
    count = len(arrays)
    return pl.pallas_call(
        nothing,
        in_specs=[ANY] * count,
        out_specs=[ANY] * count,
        out_shape=[jax.ShapeDtypeStruct(a.shape, a.dtype) for a in arrays],
        input_output_aliases={i: i for i in range(count)},
        name="together",
    )(*arrays)


def gather_tree(own, up, down, pair, tie=False):
    half = own.shape[0] // 2
    below, above, beside = up(own), down(own), pair(own)
    if tie:
        above, beside = together(above, beside)
    below_beside, above_beside, far = pair(below), down(beside), up(below)
    far_beside = [(0, down(above_beside[:half])), (half, up(below_beside[half:]))]
    whole = {
        (0, 0): own,
        (-1, 0): below,
        (1, 0): above,
        (0, 1): beside,
        (-1, 1): below_beside,
        (1, 1): above_beside,
        (2, 0): far,
    }
    return [far_beside if place == (2, 1) else [(0, whole[place])] for place in PLACES]


def scatter_first(corner, blocks, up, down, *later):
    low, high = (part.astype(BF16) for part in corner)
    half = low.shape[0]
    none = ((0, 0), (0, 0))
    low, high, *later = together(up(low), down(high), *later)
    above_beside = blocks[1, 1].astype(F32) + jnp.pad(low.astype(F32), ((0, half), *none))
    below_beside = blocks[-1, 1].astype(F32) + jnp.pad(high.astype(F32), ((half, 0), *none))
    leaving = (above_beside.astype(BF16), below_beside.astype(BF16), blocks[2, 0].astype(BF16))
    return leaving, *later


def scatter_second(leaving, blocks, up, down, pair):
    above_beside, below_beside, far = leaving
    below = blocks[-1, 0].astype(F32) + pair(below_beside).astype(F32) + down(far).astype(F32)
    beside = blocks[0, 1].astype(F32) + up(above_beside).astype(F32)
    return below.astype(BF16), beside.astype(BF16), blocks[1, 0].astype(BF16)


def scatter_third(leaving, own, up, down, pair):
    below, beside, above = leaving
    return (
        own.astype(F32)
        + up(above).astype(F32)
        + down(below).astype(F32)
        + pair(beside).astype(F32)
    )


def run_list(first, last, tile_list, panel_list, key_list, multiply, acc_ref):
    def add_group(g, carry):
        products = [
            multiply(tile_list[g * GROUP + j], panel_list[g * GROUP + j]) for j in range(GROUP)
        ]
        for j in range(GROUP):
            acc_ref[key_list[g * GROUP + j]] += products[j]
        return carry

    lax.fori_loop(first, last, add_group, 0)


def zero_all(acc_ref):
    def zero(i, carry):
        acc_ref[i] = jnp.zeros(acc_ref.shape[1:], F32)
        return carry

    lax.fori_loop(0, acc_ref.shape[0], zero, 0)


def fill_tail(count, spare, tile_list, panel_list, key_list):
    for j in range(GROUP):
        tile_list[count + j] = 0
        panel_list[count + j] = 0
        key_list[count + j] = spare


def load_sources(layout, order_ref, tiles_ref, shard_refs, tiles_v, shards_v, tile_sem, part_sem, slots, col_tiles):
    copies, part = [], 0
    for i, firsts in enumerate(layout):
        own = [
            pltpu.make_async_copy(
                tiles_ref.at[order_ref[i]], tiles_v.at[pl.ds(i * slots, slots)], tile_sem.at[i]
            )
        ]
        for first in firsts:
            size = shard_refs[part].shape[0]
            own.append(
                pltpu.make_async_copy(
                    shard_refs[part],
                    shards_v.at[pl.ds(i * col_tiles + first, size)],
                    part_sem.at[part],
                )
            )
            part += 1
        for copy in own:
            copy.start()
        copies.append(own)
    return copies


def forward_products(copies, order_ref, rows_ref, cols_ref, counts_ref, tiles_v, shards_v, acc_ref, tile_list, panel_list, key_list):
    sources = len(copies)
    slots = rows_ref.shape[1]
    col_tiles = shards_v.shape[0] // sources
    spare = acc_ref.shape[0] - 1
    count, ends = jnp.int32(0), []
    for i in range(sources):
        source = order_ref[i]

        def enlist(k, count, i=i, source=source):
            tile_list[count] = i * slots + k
            panel_list[count] = i * col_tiles + cols_ref[source, k]
            key_list[count] = rows_ref[source, k]
            return count + 1

        count = lax.fori_loop(0, counts_ref[source], enlist, count)
        ends.append(count)
    fill_tail(count, spare, tile_list, panel_list, key_list)

    def multiply(tile, panel):
        return jnp.dot(tiles_v[tile], shards_v[panel], preferred_element_type=F32)

    lists = (tile_list, panel_list, key_list, multiply, acc_ref)
    half = sources // 2
    for own in copies[:half]:
        for copy in own:
            copy.wait()
    middle = ends[half - 1] // GROUP
    run_list(0, middle, *lists)
    for own in copies[half:]:
        for copy in own:
            copy.wait()
    run_list(middle, (count + GROUP - 1) // GROUP, *lists)


def forward_kernel(layout, order_ref, dest_ref, rows_ref, cols_ref, counts_ref, tiles_ref, *refs):
    parts = sum(len(firsts) for firsts in layout)
    shard_refs, refs = refs[:parts], refs[parts:]
    out_refs, offset_ref, refs = refs[: len(PLACES) + 1], refs[len(PLACES) + 1], refs[len(PLACES) + 2 :]
    acc_ref, tiles_v, shards_v, *lists, tile_sem, part_sem = refs
    slots, col_tiles = rows_ref.shape[1], shards_v.shape[0] // len(layout)
    row_tiles = acc_ref.shape[0] - 1
    copies = load_sources(
        layout, order_ref, tiles_ref, shard_refs, tiles_v, shards_v, tile_sem, part_sem, slots, col_tiles
    )
    zero_all(acc_ref)
    forward_products(
        copies, order_ref, rows_ref, cols_ref, counts_ref, tiles_v, shards_v, acc_ref, *lists
    )

    def total(i, carry):
        return carry + jnp.sum(acc_ref[i].reshape(-1, 8, acc_ref.shape[2]), axis=0)

    sums = lax.fori_loop(0, row_tiles, total, jnp.zeros((8, acc_ref.shape[2]), F32))
    offset = jnp.sum(sums, axis=0, keepdims=True) / (row_tiles * acc_ref.shape[1])
    offset_ref[...] = offset
    half = col_tiles // 2
    spans = [(out_refs[0], 0, 0, half), (out_refs[1], 0, half, half)]
    spans += [(out_refs[d + 1], d, 0, col_tiles) for d in range(1, len(PLACES))]
    for out_ref, d, first, size in spans:
        base = dest_ref[d] * col_tiles + first

        def put(i, carry, out_ref=out_ref, base=base):
            out_ref[i] = (acc_ref[base + i] - offset).astype(BF16)
            return carry

        lax.fori_loop(0, size, put, 0)


def list_shapes(cap):
    return [pltpu.SMEM((cap,), jnp.int32)] * 3


def forward_tiles(order, dests, scalars, tiles, shards):
    arrays = [array for parts in shards for _, array in parts]
    layout = tuple(tuple(first for first, _ in parts) for parts in shards)
    sources, slots, tile, _ = tiles.shape
    width = arrays[0].shape[2]
    col_tiles = sum(array.shape[0] for _, array in shards[0])
    row_tiles = col_tiles * len(PLACES)
    sizes = [col_tiles // 2] * 2 + [col_tiles] * (len(PLACES) - 1)
    out_shape = [jax.ShapeDtypeStruct((size, tile, width), BF16) for size in sizes]
    out_shape.append(jax.ShapeDtypeStruct((1, width), F32))
    return pl.pallas_call(
        functools.partial(forward_kernel, layout),
        in_specs=[SMEM] * 5 + [ANY] * (1 + len(arrays)),
        out_specs=[VMEM] * len(out_shape),
        out_shape=out_shape,
        scratch_shapes=[
            pltpu.VMEM((row_tiles + 1, tile, width), F32),
            pltpu.VMEM((sources * slots, tile, tile), BF16),
            pltpu.VMEM((sources * col_tiles, tile, width), BF16),
            *list_shapes(sources * slots + GROUP),
            pltpu.SemaphoreType.DMA((sources,)),
            pltpu.SemaphoreType.DMA((len(arrays),)),
        ],
        compiler_params=pltpu.CompilerParams(vmem_limit_bytes=VMEM_LIMIT),
        cost_estimate=pl.CostEstimate(flops=6 * 10**9, bytes_accessed=30 * 2**20, transcendentals=0),
        name="forward_tiles",
    )(order, dests, *scalars, tiles, *arrays)


def backward_kernel(layout, sizes, waits, order_ref, dest_ref, rows_ref, cols_ref, counts_ref, tiles_ref, *refs):
    parts = sum(len(firsts) for firsts in layout)
    grad_refs, refs = refs[:parts], refs[parts + waits :]
    out_refs, refs = refs[: len(sizes)], refs[len(sizes) :]
    tiles_v, grads_v, acc_ref, tile_list, panel_list, key_list, tile_sem, part_sem = refs
    slots = rows_ref.shape[1]
    sources = tiles_v.shape[0] // slots
    col_tiles = (acc_ref.shape[0] - 1) // sources

    copies, part = [], 0
    for i, firsts in enumerate(layout):
        base = dest_ref[i] * col_tiles
        for first in firsts:
            size = grad_refs[part].shape[0]
            copies.append(
                pltpu.make_async_copy(
                    grad_refs[part], grads_v.at[pl.ds(base + first, size)], part_sem.at[part]
                )
            )
            part += 1
    tile_copies = [
        pltpu.make_async_copy(
            tiles_ref.at[order_ref[i]], tiles_v.at[pl.ds(i * slots, slots)], tile_sem.at[i]
        )
        for i in range(sources)
    ]
    for copy in copies + tile_copies:
        copy.start()

    zero_all(acc_ref)
    count, ends = jnp.int32(0), []
    for i in range(sources):
        source = order_ref[i]

        def enlist(k, count, i=i, source=source):
            tile_list[count] = i * slots + k
            panel_list[count] = rows_ref[source, k]
            key_list[count] = i * col_tiles + cols_ref[source, k]
            return count + 1

        count = lax.fori_loop(0, counts_ref[source], enlist, count)
        ends.append(count)
    fill_tail(count, sources * col_tiles, tile_list, panel_list, key_list)

    def multiply(tile, panel):
        return lax.dot_general(
            tiles_v[tile], grads_v[panel], (((0,), (0,)), ((), ())), preferred_element_type=F32
        )

    lists = (tile_list, panel_list, key_list, multiply, acc_ref)
    for copy in copies + tile_copies[: sources // 2]:
        copy.wait()
    middle = ends[sources // 2 - 1] // GROUP
    run_list(0, middle, *lists)
    for copy in tile_copies[sources // 2 :]:
        copy.wait()
    run_list(middle, (count + GROUP - 1) // GROUP, *lists)

    base = 0
    for out_ref, size in zip(out_refs, sizes):

        def put(t, carry, out_ref=out_ref, base=base):
            out_ref[t] = acc_ref[base + t].astype(BF16)
            return carry

        lax.fori_loop(0, size, put, 0)
        base += size


def backward_tiles(sizes, order, dests, scalars, tiles, grads, after=()):
    arrays = [array for parts in grads for _, array in parts]
    layout = tuple(tuple(first for first, _ in parts) for parts in grads)
    slots, tile = tiles.shape[1:3]
    width = arrays[0].shape[2]
    row_tiles = sum(array.shape[0] for array in arrays)
    sources = order.shape[0]
    return pl.pallas_call(
        functools.partial(backward_kernel, layout, sizes, len(after)),
        in_specs=[SMEM] * 5 + [ANY] * (1 + len(arrays) + len(after)),
        out_specs=[VMEM] * len(sizes),
        out_shape=[jax.ShapeDtypeStruct((size, tile, width), BF16) for size in sizes],
        scratch_shapes=[
            pltpu.VMEM((sources * slots, tile, tile), BF16),
            pltpu.VMEM((row_tiles, tile, width), BF16),
            pltpu.VMEM((sum(sizes) + 1, tile, width), F32),
            *list_shapes(sources * slots + GROUP),
            pltpu.SemaphoreType.DMA((sources,)),
            pltpu.SemaphoreType.DMA((len(arrays),)),
        ],
        compiler_params=pltpu.CompilerParams(vmem_limit_bytes=VMEM_LIMIT),
        cost_estimate=pl.CostEstimate(flops=8 * 10**9, bytes_accessed=20 * 2**20, transcendentals=0),
        name="backward_tiles",
    )(order, dests, *scalars, tiles, *arrays, *after)


def sum_first_kernel(value_ref, *refs):
    refs[-1][...] = jnp.sum(value_ref[...], axis=0)


def sum_first(value, after):
    return pl.pallas_call(
        sum_first_kernel,
        in_specs=[VMEM] + [ANY] * len(after),
        out_specs=VMEM,
        out_shape=jax.ShapeDtypeStruct(value.shape[1:], value.dtype),
        name="sum_first",
    )(value, *after)


def weight_kernel(aggregate_ref, grad_ref, offset_ref, *refs):
    grads = grad_ref[...]
    sums = jnp.sum(grads.astype(F32), axis=0, keepdims=True)
    refs[-1][...] = (
        lax.dot_general(
            aggregate_ref[...], grads, (((0,), (0,)), ((), ())), preferred_element_type=F32
        )
        + offset_ref[...] * sums
    )


def weight_terms(aggregate, grads, offset, after):
    width = grads.shape[1]
    return pl.pallas_call(
        weight_kernel,
        in_specs=[VMEM] * 3 + [ANY] * len(after),
        out_specs=VMEM,
        out_shape=jax.ShapeDtypeStruct((width, width), F32),
        name="weight_terms",
    )(aggregate, grads, jnp.broadcast_to(offset[:, None], (width, width)), *after)


def copies_of_all(value, axis):
    count = lax.axis_size(axis)
    return lax.all_to_all(jnp.broadcast_to(value[None], (count, *value.shape)), axis, 0, 0)


def on_device(
    features,
    weight,
    norm_gain,
    norm_shift,
    tile_values,
    tile_rows,
    tile_cols,
    tile_counts,
    cotangent,
):
    tiles, rows, cols, counts = tile_values[0], tile_rows[0], tile_cols[0], tile_counts[0]
    local_rows, width = features.shape
    tile = tiles.shape[-1]
    col_tiles = local_rows // tile
    blk_count = lax.axis_size("blk")
    rep_count = lax.axis_size("rep")
    node_count = local_rows * blk_count * rep_count
    blk, rep = lax.axis_index("blk"), lax.axis_index("rep")
    z, y_low, core = blk // 4, (blk // 2) % 2, blk % 2
    y_high, x = rep // RING, rep % RING
    own_core = jnp.stack([blk_index(z + a + RING, y_low + b, core) for a, b in PLACES])
    other_core = own_core + (1 - 2 * core)
    dests = jnp.stack([rep_index(x + a + RING, y_high + b) for a, b in PLACES])
    *blk_tree, across = blk_links()
    rep_tree = rep_links()

    mine = gather_tree(features.reshape(col_tiles, tile, width), *blk_tree)
    theirs = [[(first, across(array)) for first, array in parts] for parts in mine]
    backwards = slice(None, None, -1)
    scalars = (rows, cols, counts)
    order = jnp.stack([own_core[backwards], other_core[backwards]], axis=1).reshape(-1)
    shards = [parts for both in zip(mine[backwards], theirs[backwards]) for parts in both]
    up, down, pair = rep_tree
    low, high, *rest, offset = forward_tiles(order, dests, scalars, tiles, shards)
    blocks = dict(zip(PLACES[1:], rest))
    [leaving] = scatter_first((low, high), blocks, up, down)
    leaving = scatter_second(leaving, blocks, *rep_tree)
    shifted = scatter_third(leaving, blocks[0, 0], *rep_tree).reshape(local_rows, width)
    aggregate = shifted.astype(BF16)
    projected = jnp.dot(aggregate, weight, preferred_element_type=F32)
    own_mean = jnp.sum(projected, axis=0) / local_rows
    own_square = jnp.sum((projected - own_mean) ** 2, axis=0)
    everyone = copies_of_all(jnp.stack([own_mean, own_square, offset[0]]), ("blk", "rep"))
    everyone = everyone.reshape(blk_count, rep_count, 3, width)
    offsets = jnp.sum(everyone[:, :, 2], axis=1)
    moves = jnp.dot(offsets, weight.astype(F32), precision=lax.Precision.HIGHEST)
    means = everyone[:, :, 0] + moves[:, None]
    feat_mean = jnp.sum(means, axis=(0, 1)) / (blk_count * rep_count)
    square_sum = jnp.sum(everyone[:, :, 1], axis=(0, 1)) + local_rows * jnp.sum(
        (means - feat_mean) ** 2, axis=(0, 1)
    )
    group_moved = lax.dynamic_index_in_dim(moves, blk, 0, keepdims=False)
    group_offset = lax.dynamic_index_in_dim(offsets, blk, 0, keepdims=False)
    inv_std = lax.rsqrt(square_sum / node_count + norm_eps)
    normed = (projected + (group_moved - feat_mean)) * inv_std
    affine = norm_gain * normed + norm_shift
    gate_value = jax.nn.sigmoid(affine)
    output = (affine * gate_value).astype(BF16)
    grad_affine = cotangent.astype(F32) * gate_value * (1.0 + affine * (1.0 - gate_value))
    grad_beta, grad_gamma = jnp.sum(
        copies_of_all(
            jnp.stack([jnp.sum(grad_affine, axis=0), jnp.sum(grad_affine * normed, axis=0)]),
            ("blk", "rep"),
        ),
        axis=0,
    )
    grad_summed = (
        norm_gain
        * inv_std
        * (grad_affine - grad_beta / node_count - normed * grad_gamma / node_count)
    ).astype(BF16)

    sent = lax.dot_general(
        grad_summed, weight, (((1,), (1,)), ((), ())), preferred_element_type=F32
    ).astype(BF16)
    grads = gather_tree(sent.reshape(col_tiles, tile, width), *rep_tree, tie=True)
    arrived = {place: parts[0][1] for place, parts in zip(PLACES, grads)}
    weight_term = weight_terms(aggregate, grad_summed, group_offset, [arrived[1, 0]])
    pieces = lax.all_to_all(weight_term.reshape(blk_count, -1, width), "blk", 0, 0)
    piece = sum_first(pieces, [arrived[-1, 1]])

    half = col_tiles // 2
    sizes = (half, half, *(col_tiles,) * (len(PLACES) - 1))
    arrays = backward_tiles(
        sizes * 2,
        jnp.concatenate([other_core, own_core]),
        dests,
        scalars,
        tiles,
        grads,
        [piece],
    )
    given, kept = arrays[: len(sizes)], arrays[len(sizes) :]
    low, high, *rest = [b.astype(F32) + across(a).astype(F32) for a, b in zip(given, kept)]
    products = dict(zip(PLACES[1:], rest))
    up, down, pair = blk_tree
    leaving, piece = scatter_first((low, high), products, up, down, piece)
    terms = copies_of_all(piece, "rep")
    below, beside, above = scatter_second(leaving, products, *blk_tree)
    beside, terms = together(beside, terms)
    grad_x = scatter_third((below, beside, above), products[0, 0], *blk_tree).astype(BF16)
    grad_w = copies_of_all(jnp.sum(terms, axis=0), "blk").reshape(weight.shape)
    return (output, grad_x.reshape(local_rows, width), grad_w, grad_gamma, grad_beta)


def solution(mesh):
    return jax.shard_map(
        on_device,
        mesh=mesh,
        in_specs=(
            P(("blk", "rep"), None),
            P(),
            P(),
            P(),
            P("blk", "rep", None, None, None),
            P("blk", "rep", None),
            P("blk", "rep", None),
            P("blk", "rep"),
            P(("blk", "rep"), None),
        ),
        out_specs=(P(("blk", "rep"), None), P(("blk", "rep"), None), P(), P(), P()),
        check_vma=False,
    )
```

```python
import functools

import jax
import jax.numpy as jnp
from jax import lax
from jax.experimental import pallas as pl
from jax.experimental.pallas import tpu as pltpu
from jax.sharding import PartitionSpec as P

norm_eps = 1e-05
GROUP = 32
BF16, F32 = jnp.bfloat16, jnp.float32
VMEM_LIMIT = 60 * 2**20
RING = 4
PLACES = ((2, 1), (1, 1), (-1, 1), (2, 0), (0, 1), (1, 0), (-1, 0), (0, 0))
ANY = pl.BlockSpec(memory_space=pl.ANY)
VMEM = pl.BlockSpec(memory_space=pltpu.VMEM)
SMEM = pl.BlockSpec(memory_space=pltpu.SMEM)


def blk_index(z, y, core):
    return (z % RING) * 4 + (y % 2) * 2 + core % 2


def rep_index(x, y):
    return (y % 2) * RING + x % RING


def blk_links():
    spots = [(z, y, c) for z in range(RING) for y in range(2) for c in range(2)]

    def link(dz, dy, dc):
        pairs = [(blk_index(z, y, c), blk_index(z + dz, y + dy, c + dc)) for z, y, c in spots]
        return lambda value: lax.ppermute(value, "blk", pairs)

    return link(1, 0, 0), link(-1, 0, 0), link(0, 1, 0), link(0, 0, 1)


def rep_links():
    spots = [(x, y) for x in range(RING) for y in range(2)]

    def link(dx, dy):
        pairs = [(rep_index(x, y), rep_index(x + dx, y + dy)) for x, y in spots]
        return lambda value: lax.ppermute(value, "rep", pairs)

    return link(1, 0), link(-1, 0), link(0, 1)


def nothing(*refs):
    pass


def together(*arrays):
    count = len(arrays)
    return pl.pallas_call(
        nothing,
        in_specs=[ANY] * count,
        out_specs=[ANY] * count,
        out_shape=[jax.ShapeDtypeStruct(a.shape, a.dtype) for a in arrays],
        input_output_aliases={i: i for i in range(count)},
        name="together",
    )(*arrays)


def cuts(tiles):
    return 3 * tiles // 8, 6 * tiles // 8


def gather_tree(own, up, down, pair, tie=None):
    a, b = cuts(own.shape[0])
    below, above, beside = up(own), down(own), pair(own)
    if tie is not None:
        above, beside, tie = together(above, beside, tie)
    below_beside, above_beside, far = pair(below), down(beside), up(below)
    far_beside = [(0, pair(far[:a])), (a, down(above_beside[a:b])), (b, up(below_beside[b:]))]
    whole = {
        (0, 0): own,
        (-1, 0): below,
        (1, 0): above,
        (0, 1): beside,
        (-1, 1): below_beside,
        (1, 1): above_beside,
        (2, 0): far,
    }
    return [far_beside if place == (2, 1) else [(0, whole[place])] for place in PLACES], tie


def placed(part, first, tiles):
    return jnp.pad(part.astype(F32), ((first, tiles - first - part.shape[0]), (0, 0), (0, 0)))


def scatter_first(corner, blocks, up, down, pair, *later):
    low, middle, high = (part.astype(BF16) for part in corner)
    tiles = blocks[2, 0].shape[0]
    a, b = cuts(tiles)
    low, middle, high, *later = together(pair(low), up(middle), down(high), *later)
    far = blocks[2, 0].astype(F32) + placed(low, 0, tiles)
    above_beside = blocks[1, 1].astype(F32) + placed(middle, a, tiles)
    below_beside = blocks[-1, 1].astype(F32) + placed(high, b, tiles)
    return (above_beside.astype(BF16), below_beside.astype(BF16), far.astype(BF16)), *later


def scatter_second(leaving, blocks, up, down, pair):
    above_beside, below_beside, far = leaving
    below = blocks[-1, 0].astype(F32) + pair(below_beside).astype(F32) + down(far).astype(F32)
    beside = blocks[0, 1].astype(F32) + up(above_beside).astype(F32)
    return below.astype(BF16), beside.astype(BF16), blocks[1, 0].astype(BF16)


def scatter_third(leaving, own, up, down, pair):
    below, beside, above = leaving
    return (
        own.astype(F32)
        + up(above).astype(F32)
        + down(below).astype(F32)
        + pair(beside).astype(F32)
    )


def run_list(first, last, tile_list, panel_list, key_list, multiply, acc_ref):
    def add_group(g, carry):
        products = [
            multiply(tile_list[g * GROUP + j], panel_list[g * GROUP + j]) for j in range(GROUP)
        ]
        for j in range(GROUP):
            acc_ref[key_list[g * GROUP + j]] += products[j]
        return carry

    lax.fori_loop(first, last, add_group, 0)


def zero_all(acc_ref):
    def zero(i, carry):
        acc_ref[i] = jnp.zeros(acc_ref.shape[1:], F32)
        return carry

    lax.fori_loop(0, acc_ref.shape[0], zero, 0)


def fill_tail(count, spare, tile_list, panel_list, key_list):
    for j in range(GROUP):
        tile_list[count + j] = 0
        panel_list[count + j] = 0
        key_list[count + j] = spare


def load_sources(layout, order_ref, tiles_ref, shard_refs, tiles_v, shards_v, tile_sem, part_sem, slots, col_tiles):
    copies, part = [], 0
    for i, firsts in enumerate(layout):
        own = [
            pltpu.make_async_copy(
                tiles_ref.at[order_ref[i]], tiles_v.at[pl.ds(i * slots, slots)], tile_sem.at[i]
            )
        ]
        for first in firsts:
            size = shard_refs[part].shape[0]
            own.append(
                pltpu.make_async_copy(
                    shard_refs[part],
                    shards_v.at[pl.ds(i * col_tiles + first, size)],
                    part_sem.at[part],
                )
            )
            part += 1
        for copy in own:
            copy.start()
        copies.append(own)
    return copies


def forward_products(copies, order_ref, rows_ref, cols_ref, counts_ref, tiles_v, shards_v, acc_ref, tile_list, panel_list, key_list):
    sources = len(copies)
    slots = rows_ref.shape[1]
    col_tiles = shards_v.shape[0] // sources
    spare = acc_ref.shape[0] - 1
    count, ends = jnp.int32(0), []
    for i in range(sources):
        source = order_ref[i]

        def enlist(k, count, i=i, source=source):
            tile_list[count] = i * slots + k
            panel_list[count] = i * col_tiles + cols_ref[source, k]
            key_list[count] = rows_ref[source, k]
            return count + 1

        count = lax.fori_loop(0, counts_ref[source], enlist, count)
        ends.append(count)
    fill_tail(count, spare, tile_list, panel_list, key_list)

    def multiply(tile, panel):
        return jnp.dot(tiles_v[tile], shards_v[panel], preferred_element_type=F32)

    lists = (tile_list, panel_list, key_list, multiply, acc_ref)
    half = sources // 2
    for own in copies[:half]:
        for copy in own:
            copy.wait()
    middle = ends[half - 1] // GROUP
    run_list(0, middle, *lists)
    for own in copies[half:]:
        for copy in own:
            copy.wait()
    run_list(middle, (count + GROUP - 1) // GROUP, *lists)


def forward_kernel(layout, order_ref, dest_ref, rows_ref, cols_ref, counts_ref, tiles_ref, *refs):
    parts = sum(len(firsts) for firsts in layout)
    shard_refs, refs = refs[:parts], refs[parts:]
    outs = len(PLACES) + 2
    out_refs, offset_ref, refs = refs[:outs], refs[outs], refs[outs + 1 :]
    acc_ref, tiles_v, shards_v, *lists, tile_sem, part_sem = refs
    slots, col_tiles = rows_ref.shape[1], shards_v.shape[0] // len(layout)
    row_tiles = acc_ref.shape[0] - 1
    copies = load_sources(
        layout, order_ref, tiles_ref, shard_refs, tiles_v, shards_v, tile_sem, part_sem, slots, col_tiles
    )
    zero_all(acc_ref)
    forward_products(
        copies, order_ref, rows_ref, cols_ref, counts_ref, tiles_v, shards_v, acc_ref, *lists
    )

    def total(i, carry):
        return carry + jnp.sum(acc_ref[i].reshape(-1, 8, acc_ref.shape[2]), axis=0)

    sums = lax.fori_loop(0, row_tiles, total, jnp.zeros((8, acc_ref.shape[2]), F32))
    offset = jnp.sum(sums, axis=0, keepdims=True) / (row_tiles * acc_ref.shape[1])
    offset_ref[...] = offset
    a, b = cuts(col_tiles)
    spans = [(out_refs[0], 0, 0, a), (out_refs[1], 0, a, b - a), (out_refs[2], 0, b, col_tiles - b)]
    spans += [(out_refs[d + 2], d, 0, col_tiles) for d in range(1, len(PLACES))]
    for out_ref, d, first, size in spans:
        base = dest_ref[d] * col_tiles + first

        def put(i, carry, out_ref=out_ref, base=base):
            out_ref[i] = (acc_ref[base + i] - offset).astype(BF16)
            return carry

        lax.fori_loop(0, size, put, 0)


def block_sizes(tiles):
    a, b = cuts(tiles)
    return (a, b - a, tiles - b, *(tiles,) * (len(PLACES) - 1))


def list_shapes(cap):
    return [pltpu.SMEM((cap,), jnp.int32)] * 3


def forward_tiles(order, dests, scalars, tiles, shards):
    arrays = [array for parts in shards for _, array in parts]
    layout = tuple(tuple(first for first, _ in parts) for parts in shards)
    sources, slots, tile, _ = tiles.shape
    width = arrays[0].shape[2]
    col_tiles = sum(array.shape[0] for _, array in shards[0])
    row_tiles = col_tiles * len(PLACES)
    sizes = block_sizes(col_tiles)
    out_shape = [jax.ShapeDtypeStruct((size, tile, width), BF16) for size in sizes]
    out_shape.append(jax.ShapeDtypeStruct((1, width), F32))
    return pl.pallas_call(
        functools.partial(forward_kernel, layout),
        in_specs=[SMEM] * 5 + [ANY] * (1 + len(arrays)),
        out_specs=[VMEM] * len(out_shape),
        out_shape=out_shape,
        scratch_shapes=[
            pltpu.VMEM((row_tiles + 1, tile, width), F32),
            pltpu.VMEM((sources * slots, tile, tile), BF16),
            pltpu.VMEM((sources * col_tiles, tile, width), BF16),
            *list_shapes(sources * slots + GROUP),
            pltpu.SemaphoreType.DMA((sources,)),
            pltpu.SemaphoreType.DMA((len(arrays),)),
        ],
        compiler_params=pltpu.CompilerParams(vmem_limit_bytes=VMEM_LIMIT),
        cost_estimate=pl.CostEstimate(flops=6 * 10**9, bytes_accessed=30 * 2**20, transcendentals=0),
        name="forward_tiles",
    )(order, dests, *scalars, tiles, *arrays)


def backward_kernel(layout, sizes, waits, order_ref, dest_ref, rows_ref, cols_ref, counts_ref, tiles_ref, *refs):
    parts = sum(len(firsts) for firsts in layout)
    grad_refs, refs = refs[:parts], refs[parts + waits :]
    out_refs, refs = refs[: len(sizes)], refs[len(sizes) :]
    tiles_v, grads_v, acc_ref, tile_list, panel_list, key_list, tile_sem, part_sem = refs
    slots = rows_ref.shape[1]
    sources = tiles_v.shape[0] // slots
    col_tiles = (acc_ref.shape[0] - 1) // sources

    copies, part = [], 0
    for i, firsts in enumerate(layout):
        base = dest_ref[i] * col_tiles
        for first in firsts:
            size = grad_refs[part].shape[0]
            copies.append(
                pltpu.make_async_copy(
                    grad_refs[part], grads_v.at[pl.ds(base + first, size)], part_sem.at[part]
                )
            )
            part += 1
    tile_copies = [
        pltpu.make_async_copy(
            tiles_ref.at[order_ref[i]], tiles_v.at[pl.ds(i * slots, slots)], tile_sem.at[i]
        )
        for i in range(sources)
    ]
    for copy in copies + tile_copies:
        copy.start()

    zero_all(acc_ref)
    count, ends = jnp.int32(0), []
    for i in range(sources):
        source = order_ref[i]

        def enlist(k, count, i=i, source=source):
            tile_list[count] = i * slots + k
            panel_list[count] = rows_ref[source, k]
            key_list[count] = i * col_tiles + cols_ref[source, k]
            return count + 1

        count = lax.fori_loop(0, counts_ref[source], enlist, count)
        ends.append(count)
    fill_tail(count, sources * col_tiles, tile_list, panel_list, key_list)

    def multiply(tile, panel):
        return lax.dot_general(
            tiles_v[tile], grads_v[panel], (((0,), (0,)), ((), ())), preferred_element_type=F32
        )

    lists = (tile_list, panel_list, key_list, multiply, acc_ref)
    for copy in copies + tile_copies[: sources // 2]:
        copy.wait()
    middle = ends[sources // 2 - 1] // GROUP
    run_list(0, middle, *lists)
    for copy in tile_copies[sources // 2 :]:
        copy.wait()
    run_list(middle, (count + GROUP - 1) // GROUP, *lists)

    base = 0
    for out_ref, size in zip(out_refs, sizes):

        def put(t, carry, out_ref=out_ref, base=base):
            out_ref[t] = acc_ref[base + t].astype(BF16)
            return carry

        lax.fori_loop(0, size, put, 0)
        base += size


def backward_tiles(sizes, order, dests, scalars, tiles, grads, after=()):
    arrays = [array for parts in grads for _, array in parts]
    layout = tuple(tuple(first for first, _ in parts) for parts in grads)
    slots, tile = tiles.shape[1:3]
    width = arrays[0].shape[2]
    row_tiles = sum(array.shape[0] for array in arrays)
    sources = order.shape[0]
    return pl.pallas_call(
        functools.partial(backward_kernel, layout, sizes, len(after)),
        in_specs=[SMEM] * 5 + [ANY] * (1 + len(arrays) + len(after)),
        out_specs=[VMEM] * len(sizes),
        out_shape=[jax.ShapeDtypeStruct((size, tile, width), BF16) for size in sizes],
        scratch_shapes=[
            pltpu.VMEM((sources * slots, tile, tile), BF16),
            pltpu.VMEM((row_tiles, tile, width), BF16),
            pltpu.VMEM((sum(sizes) + 1, tile, width), F32),
            *list_shapes(sources * slots + GROUP),
            pltpu.SemaphoreType.DMA((sources,)),
            pltpu.SemaphoreType.DMA((len(arrays),)),
        ],
        compiler_params=pltpu.CompilerParams(vmem_limit_bytes=VMEM_LIMIT),
        cost_estimate=pl.CostEstimate(flops=8 * 10**9, bytes_accessed=20 * 2**20, transcendentals=0),
        name="backward_tiles",
    )(order, dests, *scalars, tiles, *arrays, *after)


def weight_kernel(aggregate_ref, grad_ref, offset_ref, *refs):
    grads = grad_ref[...]
    sums = jnp.sum(grads.astype(F32), axis=0, keepdims=True)
    refs[-1][...] = (
        lax.dot_general(
            aggregate_ref[...], grads, (((0,), (0,)), ((), ())), preferred_element_type=F32
        )
        + offset_ref[...] * sums
    )


def weight_terms(aggregate, grads, offset, after):
    width = grads.shape[1]
    return pl.pallas_call(
        weight_kernel,
        in_specs=[VMEM] * 3 + [ANY] * len(after),
        out_specs=VMEM,
        out_shape=jax.ShapeDtypeStruct((width, width), F32),
        name="weight_terms",
    )(aggregate, grads, jnp.broadcast_to(offset[:, None], (width, width)), *after)


def copies_of_all(value, axis):
    count = lax.axis_size(axis)
    return lax.all_to_all(jnp.broadcast_to(value[None], (count, *value.shape)), axis, 0, 0)


def on_device(
    features,
    weight,
    norm_gain,
    norm_shift,
    tile_values,
    tile_rows,
    tile_cols,
    tile_counts,
    cotangent,
):
    tiles, rows, cols, counts = tile_values[0], tile_rows[0], tile_cols[0], tile_counts[0]
    local_rows, width = features.shape
    tile = tiles.shape[-1]
    col_tiles = local_rows // tile
    blk_count = lax.axis_size("blk")
    rep_count = lax.axis_size("rep")
    node_count = local_rows * blk_count * rep_count
    blk, rep = lax.axis_index("blk"), lax.axis_index("rep")
    z, y_low, core = blk // 4, (blk // 2) % 2, blk % 2
    y_high, x = rep // RING, rep % RING
    own_core = jnp.stack([blk_index(z + a + RING, y_low + b, core) for a, b in PLACES])
    other_core = own_core + (1 - 2 * core)
    dests = jnp.stack([rep_index(x + a + RING, y_high + b) for a, b in PLACES])
    *blk_tree, across = blk_links()
    rep_tree = rep_links()

    mine, _ = gather_tree(features.reshape(col_tiles, tile, width), *blk_tree)
    theirs = [[(first, across(array)) for first, array in parts] for parts in mine]
    backwards = slice(None, None, -1)
    scalars = (rows, cols, counts)
    order = jnp.stack([own_core[backwards], other_core[backwards]], axis=1).reshape(-1)
    shards = [parts for both in zip(mine[backwards], theirs[backwards]) for parts in both]
    *arrays, offset = forward_tiles(order, dests, scalars, tiles, shards)
    blocks = dict(zip(PLACES[1:], arrays[3:]))
    [leaving] = scatter_first(arrays[:3], blocks, *rep_tree)
    leaving = scatter_second(leaving, blocks, *rep_tree)
    shifted = scatter_third(leaving, blocks[0, 0], *rep_tree).reshape(local_rows, width)
    aggregate = shifted.astype(BF16)
    projected = jnp.dot(aggregate, weight, preferred_element_type=F32)
    group_offset = jnp.sum(copies_of_all(offset[0], "rep"), axis=0)
    moved = jnp.dot(group_offset[None], weight.astype(F32), precision=lax.Precision.HIGHEST)[0]
    own_mean = jnp.sum(projected, axis=0) / local_rows
    own_square = jnp.sum((projected - own_mean) ** 2, axis=0)
    everyone = copies_of_all(jnp.stack([own_mean + moved, own_square]), ("blk", "rep"))
    feat_mean = jnp.sum(everyone[:, 0], axis=0) / (blk_count * rep_count)
    square_sum = jnp.sum(everyone[:, 1], axis=0) + local_rows * jnp.sum(
        (everyone[:, 0] - feat_mean) ** 2, axis=0
    )
    inv_std = lax.rsqrt(square_sum / node_count + norm_eps)
    normed = (projected + (moved - feat_mean)) * inv_std
    affine = norm_gain * normed + norm_shift
    gate_value = jax.nn.sigmoid(affine)
    output = (affine * gate_value).astype(BF16)
    grad_affine = cotangent.astype(F32) * gate_value * (1.0 + affine * (1.0 - gate_value))
    grad_beta, grad_gamma = jnp.sum(
        copies_of_all(
            jnp.stack([jnp.sum(grad_affine, axis=0), jnp.sum(grad_affine * normed, axis=0)]),
            ("blk", "rep"),
        ),
        axis=0,
    )
    grad_summed = (
        norm_gain
        * inv_std
        * (grad_affine - grad_beta / node_count - normed * grad_gamma / node_count)
    ).astype(BF16)

    sent = lax.dot_general(
        grad_summed, weight, (((1,), (1,)), ((), ())), preferred_element_type=F32
    ).astype(BF16)
    weight_term = weight_terms(aggregate, grad_summed, group_offset, [])
    pieces = lax.all_to_all(weight_term.reshape(blk_count, -1, width), "blk", 0, 0)
    grads, pieces = gather_tree(sent.reshape(col_tiles, tile, width), *rep_tree, pieces)
    piece = jnp.sum(pieces, axis=0)

    sizes = block_sizes(col_tiles)
    arrays = backward_tiles(
        sizes * 2,
        jnp.concatenate([other_core, own_core]),
        dests,
        scalars,
        tiles,
        grads,
    )
    given, kept = arrays[: len(sizes)], arrays[len(sizes) :]
    arrays = [b.astype(F32) + across(a).astype(F32) for a, b in zip(given, kept)]
    products = dict(zip(PLACES[1:], arrays[3:]))
    leaving, piece = scatter_first(arrays[:3], products, *blk_tree, piece)
    terms = copies_of_all(piece, "rep")
    below, beside, above = scatter_second(leaving, products, *blk_tree)
    beside, terms = together(beside, terms)
    grad_x = scatter_third((below, beside, above), products[0, 0], *blk_tree).astype(BF16)
    grad_w = copies_of_all(jnp.sum(terms, axis=0), "blk").reshape(weight.shape)
    return (output, grad_x.reshape(local_rows, width), grad_w, grad_gamma, grad_beta)


def solution(mesh):
    return jax.shard_map(
        on_device,
        mesh=mesh,
        in_specs=(
            P(("blk", "rep"), None),
            P(),
            P(),
            P(),
            P("blk", "rep", None, None, None),
            P("blk", "rep", None),
            P("blk", "rep", None),
            P("blk", "rep"),
            P(("blk", "rep"), None),
        ),
        out_specs=(P(("blk", "rep"), None), P(("blk", "rep"), None), P(), P(), P()),
        check_vma=False,
    )
```

```python
import functools

import jax
import jax.numpy as jnp
from jax import lax
from jax.experimental import pallas as pl
from jax.experimental.pallas import tpu as pltpu
from jax.sharding import PartitionSpec as P

norm_eps = 1e-05
GROUP = 32
BF16, F32 = jnp.bfloat16, jnp.float32
VMEM_LIMIT = 60 * 2**20
RING = 4
PLACES = ((2, 1), (1, 1), (-1, 1), (2, 0), (0, 1), (1, 0), (-1, 0), (0, 0))
ANY = pl.BlockSpec(memory_space=pl.ANY)
VMEM = pl.BlockSpec(memory_space=pltpu.VMEM)
SMEM = pl.BlockSpec(memory_space=pltpu.SMEM)


def blk_index(z, y, core):
    return (z % RING) * 4 + (y % 2) * 2 + core % 2


def rep_index(x, y):
    return (y % 2) * RING + x % RING


def blk_links():
    spots = [(z, y, c) for z in range(RING) for y in range(2) for c in range(2)]

    def link(dz, dy, dc):
        pairs = [(blk_index(z, y, c), blk_index(z + dz, y + dy, c + dc)) for z, y, c in spots]
        return lambda value: lax.ppermute(value, "blk", pairs)

    return link(1, 0, 0), link(-1, 0, 0), link(0, 1, 0), link(0, 0, 1)


def rep_links():
    spots = [(x, y) for x in range(RING) for y in range(2)]

    def link(dx, dy):
        pairs = [(rep_index(x, y), rep_index(x + dx, y + dy)) for x, y in spots]
        return lambda value: lax.ppermute(value, "rep", pairs)

    return link(1, 0), link(-1, 0), link(0, 1)


def nothing(*refs):
    pass


def together(*arrays):
    count = len(arrays)
    return pl.pallas_call(
        nothing,
        in_specs=[ANY] * count,
        out_specs=[ANY] * count,
        out_shape=[jax.ShapeDtypeStruct(a.shape, a.dtype) for a in arrays],
        input_output_aliases={i: i for i in range(count)},
        name="together",
    )(*arrays)


def cuts(tiles):
    return 3 * tiles // 8, 6 * tiles // 8


def gather_tree(own, up, down, pair, first=None, second=None):
    a, b = cuts(own.shape[0])
    below, above, beside = up(own), down(own), pair(own)
    if second:
        above, beside, first = together(above, beside, first)
    below_beside, above_beside, far = pair(below), down(beside), up(below)
    if second:
        above_beside, first = together(above_beside, second(first))
    far_beside = [(0, pair(far[:a])), (a, down(above_beside[a:b])), (b, up(below_beside[b:]))]
    whole = {
        (0, 0): own,
        (-1, 0): below,
        (1, 0): above,
        (0, 1): beside,
        (-1, 1): below_beside,
        (1, 1): above_beside,
        (2, 0): far,
    }
    return [far_beside if place == (2, 1) else [(0, whole[place])] for place in PLACES], first


def placed(part, first, tiles):
    return jnp.pad(part.astype(F32), ((first, tiles - first - part.shape[0]), (0, 0), (0, 0)))


def scatter_first(corner, blocks, up, down, pair, *later):
    low, middle, high = (part.astype(BF16) for part in corner)
    tiles = blocks[2, 0].shape[0]
    a, b = cuts(tiles)
    low, middle, high, *later = together(pair(low), up(middle), down(high), *later)
    far = blocks[2, 0].astype(F32) + placed(low, 0, tiles)
    above_beside = blocks[1, 1].astype(F32) + placed(middle, a, tiles)
    below_beside = blocks[-1, 1].astype(F32) + placed(high, b, tiles)
    return (above_beside.astype(BF16), below_beside.astype(BF16), far.astype(BF16)), *later


def scatter_second(leaving, blocks, up, down, pair):
    above_beside, below_beside, far = leaving
    below = blocks[-1, 0].astype(F32) + pair(below_beside).astype(F32) + down(far).astype(F32)
    beside = blocks[0, 1].astype(F32) + up(above_beside).astype(F32)
    return below.astype(BF16), beside.astype(BF16), blocks[1, 0].astype(BF16)


def scatter_third(leaving, own, up, down, pair):
    below, beside, above = leaving
    return (
        own.astype(F32)
        + up(above).astype(F32)
        + down(below).astype(F32)
        + pair(beside).astype(F32)
    )


def run_list(first, last, tile_list, panel_list, key_list, multiply, acc_ref):
    def add_group(g, carry):
        products = [
            multiply(tile_list[g * GROUP + j], panel_list[g * GROUP + j]) for j in range(GROUP)
        ]
        for j in range(GROUP):
            acc_ref[key_list[g * GROUP + j]] += products[j]
        return carry

    lax.fori_loop(first, last, add_group, 0)


def zero_all(acc_ref):
    def zero(i, carry):
        acc_ref[i] = jnp.zeros(acc_ref.shape[1:], F32)
        return carry

    lax.fori_loop(0, acc_ref.shape[0], zero, 0)


def fill_tail(count, spare, tile_list, panel_list, key_list):
    for j in range(GROUP):
        tile_list[count + j] = 0
        panel_list[count + j] = 0
        key_list[count + j] = spare


def load_sources(layout, order_ref, tiles_ref, shard_refs, tiles_v, shards_v, tile_sem, part_sem, slots, col_tiles):
    copies, part = [], 0
    for i, firsts in enumerate(layout):
        own = [
            pltpu.make_async_copy(
                tiles_ref.at[order_ref[i]], tiles_v.at[pl.ds(i * slots, slots)], tile_sem.at[i]
            )
        ]
        for first in firsts:
            size = shard_refs[part].shape[0]
            own.append(
                pltpu.make_async_copy(
                    shard_refs[part],
                    shards_v.at[pl.ds(i * col_tiles + first, size)],
                    part_sem.at[part],
                )
            )
            part += 1
        for copy in own:
            copy.start()
        copies.append(own)
    return copies


def forward_products(copies, order_ref, rows_ref, cols_ref, counts_ref, tiles_v, shards_v, acc_ref, tile_list, panel_list, key_list):
    sources = len(copies)
    slots = rows_ref.shape[1]
    col_tiles = shards_v.shape[0] // sources
    spare = acc_ref.shape[0] - 1
    count, ends = jnp.int32(0), []
    for i in range(sources):
        source = order_ref[i]

        def enlist(k, count, i=i, source=source):
            tile_list[count] = i * slots + k
            panel_list[count] = i * col_tiles + cols_ref[source, k]
            key_list[count] = rows_ref[source, k]
            return count + 1

        count = lax.fori_loop(0, counts_ref[source], enlist, count)
        ends.append(count)
    fill_tail(count, spare, tile_list, panel_list, key_list)

    def multiply(tile, panel):
        return jnp.dot(tiles_v[tile], shards_v[panel], preferred_element_type=F32)

    lists = (tile_list, panel_list, key_list, multiply, acc_ref)
    half = sources // 2
    for own in copies[:half]:
        for copy in own:
            copy.wait()
    middle = ends[half - 1] // GROUP
    run_list(0, middle, *lists)
    for own in copies[half:]:
        for copy in own:
            copy.wait()
    run_list(middle, (count + GROUP - 1) // GROUP, *lists)


def forward_kernel(layout, order_ref, dest_ref, rows_ref, cols_ref, counts_ref, tiles_ref, *refs):
    parts = sum(len(firsts) for firsts in layout)
    shard_refs, refs = refs[:parts], refs[parts:]
    outs = len(PLACES) + 2
    out_refs, offset_ref, refs = refs[:outs], refs[outs], refs[outs + 1 :]
    acc_ref, tiles_v, shards_v, *lists, tile_sem, part_sem = refs
    slots, col_tiles = rows_ref.shape[1], shards_v.shape[0] // len(layout)
    row_tiles = acc_ref.shape[0] - 1
    copies = load_sources(
        layout, order_ref, tiles_ref, shard_refs, tiles_v, shards_v, tile_sem, part_sem, slots, col_tiles
    )
    zero_all(acc_ref)
    forward_products(
        copies, order_ref, rows_ref, cols_ref, counts_ref, tiles_v, shards_v, acc_ref, *lists
    )

    def total(i, carry):
        return carry + jnp.sum(acc_ref[i].reshape(-1, 8, acc_ref.shape[2]), axis=0)

    sums = lax.fori_loop(0, row_tiles, total, jnp.zeros((8, acc_ref.shape[2]), F32))
    offset = jnp.sum(sums, axis=0, keepdims=True) / (row_tiles * acc_ref.shape[1])
    offset_ref[...] = offset
    a, b = cuts(col_tiles)
    spans = [(out_refs[0], 0, 0, a), (out_refs[1], 0, a, b - a), (out_refs[2], 0, b, col_tiles - b)]
    spans += [(out_refs[d + 2], d, 0, col_tiles) for d in range(1, len(PLACES))]
    for out_ref, d, first, size in spans:
        base = dest_ref[d] * col_tiles + first

        def put(i, carry, out_ref=out_ref, base=base):
            out_ref[i] = (acc_ref[base + i] - offset).astype(BF16)
            return carry

        lax.fori_loop(0, size, put, 0)


def block_sizes(tiles):
    a, b = cuts(tiles)
    return (a, b - a, tiles - b, *(tiles,) * (len(PLACES) - 1))


def list_shapes(cap):
    return [pltpu.SMEM((cap,), jnp.int32)] * 3


def forward_tiles(order, dests, scalars, tiles, shards):
    arrays = [array for parts in shards for _, array in parts]
    layout = tuple(tuple(first for first, _ in parts) for parts in shards)
    sources, slots, tile, _ = tiles.shape
    width = arrays[0].shape[2]
    col_tiles = sum(array.shape[0] for _, array in shards[0])
    row_tiles = col_tiles * len(PLACES)
    sizes = block_sizes(col_tiles)
    out_shape = [jax.ShapeDtypeStruct((size, tile, width), BF16) for size in sizes]
    out_shape.append(jax.ShapeDtypeStruct((1, width), F32))
    return pl.pallas_call(
        functools.partial(forward_kernel, layout),
        in_specs=[SMEM] * 5 + [ANY] * (1 + len(arrays)),
        out_specs=[VMEM] * len(out_shape),
        out_shape=out_shape,
        scratch_shapes=[
            pltpu.VMEM((row_tiles + 1, tile, width), F32),
            pltpu.VMEM((sources * slots, tile, tile), BF16),
            pltpu.VMEM((sources * col_tiles, tile, width), BF16),
            *list_shapes(sources * slots + GROUP),
            pltpu.SemaphoreType.DMA((sources,)),
            pltpu.SemaphoreType.DMA((len(arrays),)),
        ],
        compiler_params=pltpu.CompilerParams(vmem_limit_bytes=VMEM_LIMIT),
        cost_estimate=pl.CostEstimate(flops=6 * 10**9, bytes_accessed=30 * 2**20, transcendentals=0),
        name="forward_tiles",
    )(order, dests, *scalars, tiles, *arrays)


def backward_kernel(layout, sizes, waits, order_ref, dest_ref, rows_ref, cols_ref, counts_ref, tiles_ref, *refs):
    parts = sum(len(firsts) for firsts in layout)
    grad_refs, refs = refs[:parts], refs[parts + waits :]
    out_refs, refs = refs[: len(sizes)], refs[len(sizes) :]
    tiles_v, grads_v, acc_ref, tile_list, panel_list, key_list, tile_sem, part_sem = refs
    slots = rows_ref.shape[1]
    sources = tiles_v.shape[0] // slots
    col_tiles = (acc_ref.shape[0] - 1) // sources

    copies, part = [], 0
    for i, firsts in enumerate(layout):
        base = dest_ref[i] * col_tiles
        for first in firsts:
            size = grad_refs[part].shape[0]
            copies.append(
                pltpu.make_async_copy(
                    grad_refs[part], grads_v.at[pl.ds(base + first, size)], part_sem.at[part]
                )
            )
            part += 1
    tile_copies = [
        pltpu.make_async_copy(
            tiles_ref.at[order_ref[i]], tiles_v.at[pl.ds(i * slots, slots)], tile_sem.at[i]
        )
        for i in range(sources)
    ]
    for copy in copies + tile_copies:
        copy.start()

    zero_all(acc_ref)
    count, ends = jnp.int32(0), []
    for i in range(sources):
        source = order_ref[i]

        def enlist(k, count, i=i, source=source):
            tile_list[count] = i * slots + k
            panel_list[count] = rows_ref[source, k]
            key_list[count] = i * col_tiles + cols_ref[source, k]
            return count + 1

        count = lax.fori_loop(0, counts_ref[source], enlist, count)
        ends.append(count)
    fill_tail(count, sources * col_tiles, tile_list, panel_list, key_list)

    def multiply(tile, panel):
        return lax.dot_general(
            tiles_v[tile], grads_v[panel], (((0,), (0,)), ((), ())), preferred_element_type=F32
        )

    lists = (tile_list, panel_list, key_list, multiply, acc_ref)
    for copy in copies + tile_copies[: sources // 2]:
        copy.wait()
    middle = ends[sources // 2 - 1] // GROUP
    run_list(0, middle, *lists)
    for copy in tile_copies[sources // 2 :]:
        copy.wait()
    run_list(middle, (count + GROUP - 1) // GROUP, *lists)

    base = 0
    for out_ref, size in zip(out_refs, sizes):

        def put(t, carry, out_ref=out_ref, base=base):
            out_ref[t] = acc_ref[base + t].astype(BF16)
            return carry

        lax.fori_loop(0, size, put, 0)
        base += size


def backward_tiles(sizes, order, dests, scalars, tiles, grads, after=()):
    arrays = [array for parts in grads for _, array in parts]
    layout = tuple(tuple(first for first, _ in parts) for parts in grads)
    slots, tile = tiles.shape[1:3]
    width = arrays[0].shape[2]
    row_tiles = sum(array.shape[0] for array in arrays)
    sources = order.shape[0]
    return pl.pallas_call(
        functools.partial(backward_kernel, layout, sizes, len(after)),
        in_specs=[SMEM] * 5 + [ANY] * (1 + len(arrays) + len(after)),
        out_specs=[VMEM] * len(sizes),
        out_shape=[jax.ShapeDtypeStruct((size, tile, width), BF16) for size in sizes],
        scratch_shapes=[
            pltpu.VMEM((sources * slots, tile, tile), BF16),
            pltpu.VMEM((row_tiles, tile, width), BF16),
            pltpu.VMEM((sum(sizes) + 1, tile, width), F32),
            *list_shapes(sources * slots + GROUP),
            pltpu.SemaphoreType.DMA((sources,)),
            pltpu.SemaphoreType.DMA((len(arrays),)),
        ],
        compiler_params=pltpu.CompilerParams(vmem_limit_bytes=VMEM_LIMIT),
        cost_estimate=pl.CostEstimate(flops=8 * 10**9, bytes_accessed=20 * 2**20, transcendentals=0),
        name="backward_tiles",
    )(order, dests, *scalars, tiles, *arrays, *after)


def weight_kernel(aggregate_ref, grad_ref, offset_ref, *refs):
    grads = grad_ref[...]
    sums = jnp.sum(grads.astype(F32), axis=0, keepdims=True)
    refs[-1][...] = (
        lax.dot_general(
            aggregate_ref[...], grads, (((0,), (0,)), ((), ())), preferred_element_type=F32
        )
        + offset_ref[...] * sums
    )


def weight_terms(aggregate, grads, offset, after):
    width = grads.shape[1]
    return pl.pallas_call(
        weight_kernel,
        in_specs=[VMEM] * 3 + [ANY] * len(after),
        out_specs=VMEM,
        out_shape=jax.ShapeDtypeStruct((width, width), F32),
        name="weight_terms",
    )(aggregate, grads, jnp.broadcast_to(offset[:, None], (width, width)), *after)


def copies_of_all(value, axis):
    count = lax.axis_size(axis)
    return lax.all_to_all(jnp.broadcast_to(value[None], (count, *value.shape)), axis, 0, 0)


def on_device(
    features,
    weight,
    norm_gain,
    norm_shift,
    tile_values,
    tile_rows,
    tile_cols,
    tile_counts,
    cotangent,
):
    tiles, rows, cols, counts = tile_values[0], tile_rows[0], tile_cols[0], tile_counts[0]
    local_rows, width = features.shape
    tile = tiles.shape[-1]
    col_tiles = local_rows // tile
    blk_count = lax.axis_size("blk")
    rep_count = lax.axis_size("rep")
    node_count = local_rows * blk_count * rep_count
    blk, rep = lax.axis_index("blk"), lax.axis_index("rep")
    z, y_low, core = blk // 4, (blk // 2) % 2, blk % 2
    y_high, x = rep // RING, rep % RING
    own_core = jnp.stack([blk_index(z + a + RING, y_low + b, core) for a, b in PLACES])
    other_core = own_core + (1 - 2 * core)
    dests = jnp.stack([rep_index(x + a + RING, y_high + b) for a, b in PLACES])
    *blk_tree, across = blk_links()
    rep_tree = rep_links()

    mine, _ = gather_tree(features.reshape(col_tiles, tile, width), *blk_tree)
    theirs = [[(first, across(array)) for first, array in parts] for parts in mine]
    backwards = slice(None, None, -1)
    scalars = (rows, cols, counts)
    order = jnp.stack([own_core[backwards], other_core[backwards]], axis=1).reshape(-1)
    shards = [parts for both in zip(mine[backwards], theirs[backwards]) for parts in both]
    *arrays, offset = forward_tiles(order, dests, scalars, tiles, shards)
    blocks = dict(zip(PLACES[1:], arrays[3:]))
    [leaving] = scatter_first(arrays[:3], blocks, *rep_tree)
    leaving = scatter_second(leaving, blocks, *rep_tree)
    shifted = scatter_third(leaving, blocks[0, 0], *rep_tree).reshape(local_rows, width)
    aggregate = shifted.astype(BF16)
    projected = jnp.dot(aggregate, weight, preferred_element_type=F32)
    group_offset = jnp.sum(copies_of_all(offset[0], "rep"), axis=0)
    moved = jnp.dot(group_offset[None], weight.astype(F32), precision=lax.Precision.HIGHEST)[0]
    own_mean = jnp.sum(projected, axis=0) / local_rows
    own_square = jnp.sum((projected - own_mean) ** 2, axis=0)
    everyone = copies_of_all(jnp.stack([own_mean + moved, own_square]), ("blk", "rep"))
    feat_mean = jnp.sum(everyone[:, 0], axis=0) / (blk_count * rep_count)
    square_sum = jnp.sum(everyone[:, 1], axis=0) + local_rows * jnp.sum(
        (everyone[:, 0] - feat_mean) ** 2, axis=0
    )
    inv_std = lax.rsqrt(square_sum / node_count + norm_eps)
    normed = (projected + (moved - feat_mean)) * inv_std
    affine = norm_gain * normed + norm_shift
    gate_value = jax.nn.sigmoid(affine)
    output = (affine * gate_value).astype(BF16)
    grad_affine = cotangent.astype(F32) * gate_value * (1.0 + affine * (1.0 - gate_value))
    grad_beta, grad_gamma = jnp.sum(
        copies_of_all(
            jnp.stack([jnp.sum(grad_affine, axis=0), jnp.sum(grad_affine * normed, axis=0)]),
            ("blk", "rep"),
        ),
        axis=0,
    )
    grad_summed = (
        norm_gain
        * inv_std
        * (grad_affine - grad_beta / node_count - normed * grad_gamma / node_count)
    ).astype(BF16)

    sent = lax.dot_general(
        grad_summed, weight, (((1,), (1,)), ((), ())), preferred_element_type=F32
    ).astype(BF16)
    weight_term = weight_terms(aggregate, grad_summed, group_offset, [])
    pieces = lax.all_to_all(weight_term.reshape(blk_count, -1, width), "blk", 0, 0)
    grads, terms = gather_tree(
        sent.reshape(col_tiles, tile, width),
        *rep_tree,
        pieces,
        lambda pieces: copies_of_all(jnp.sum(pieces, axis=0), "rep"),
    )

    sizes = block_sizes(col_tiles)
    arrays = backward_tiles(
        sizes * 2,
        jnp.concatenate([other_core, own_core]),
        dests,
        scalars,
        tiles,
        grads,
    )
    given, kept = arrays[: len(sizes)], arrays[len(sizes) :]
    arrays = [b.astype(F32) + across(a).astype(F32) for a, b in zip(given, kept)]
    products = dict(zip(PLACES[1:], arrays[3:]))
    [leaving] = scatter_first(arrays[:3], products, *blk_tree)
    leaving = scatter_second(leaving, products, *blk_tree)
    grad_x = scatter_third(leaving, products[0, 0], *blk_tree).astype(BF16)
    grad_w = copies_of_all(jnp.sum(terms, axis=0), "blk").reshape(weight.shape)
    return (output, grad_x.reshape(local_rows, width), grad_w, grad_gamma, grad_beta)


def solution(mesh):
    return jax.shard_map(
        on_device,
        mesh=mesh,
        in_specs=(
            P(("blk", "rep"), None),
            P(),
            P(),
            P(),
            P("blk", "rep", None, None, None),
            P("blk", "rep", None),
            P("blk", "rep", None),
            P("blk", "rep"),
            P(("blk", "rep"), None),
        ),
        out_specs=(P(("blk", "rep"), None), P(("blk", "rep"), None), P(), P(), P()),
        check_vma=False,
    )
```
